128 devices in a mesh: band: 16 (over y, z), patch: 8 (over x, core).
Axes of the slice: x: 4, y: 4, z: 4, core: 2. Of those that a mesh axis runs over, the one named last changes fastest.
Arguments:
- grid_feat: bfloat16 [32768, 227], P(('band', 'patch')), may hold values from -6 to 6
- mesh_state: bfloat16 [32768, 512], P(('band', 'patch')), may hold values from -6 to 6
- g2m_dest: int32 [32768, 4], P(('band', 'patch')), may hold values from 0 to 127, all different within a row; in each aligned block of 256 rows (0 to 255, 256 to 511, ...) at most 16 rows name the same one
- g2m_node: int32 [32768, 4], P(('band', 'patch')), may hold values from 0 to 255
- g2m_dist: bfloat16 [32768, 4], P(('band', 'patch')), may hold values from 0.25 to 2
- mesh_src: int32 [32768, 6], P(('band', 'patch')), may hold values from 0 to 32767, as said below
- w_embed: bfloat16 [227, 512], replicated, may hold values from -0.375 to 0.375
- w_send: bfloat16 [512, 512], replicated, may hold values from -0.25 to 0.25
- w_recv: bfloat16 [512, 512], replicated, may hold values from -0.25 to 0.25
- w_node: bfloat16 [512, 512], replicated, may hold values from -0.25 to 0.25
- edge_vec: bfloat16 [512], replicated, may hold values from -4 to 4
- proc_weights: bfloat16 [2, 3, 512, 512], replicated, may hold values from -0.25 to 0.25
- cotangent: bfloat16 [32768, 512], P(('band', 'patch')), may hold values from -6 to 6
Outputs:
- mesh_out: bfloat16 [32768, 512], P(('band', 'patch'))
- mesh_grad: bfloat16 [32768, 512], P(('band', 'patch'))
- grid_grad: bfloat16 [32768, 227], P(('band', 'patch'))
The draws below stay inside these ranges and needn't reach their ends.
Inputs may be any that keep to these rules, and one draw needn't show every extreme that they name: `g2m_dest`: among the 256 grid nodes of one device's block, no device is named by more than 16 edges, and in every draw some device is named by exactly 16. The 4 devices of one grid node differ. `mesh_src`: the sender of an edge into a mesh node of device (b, p) lies on device (b, p), or among the last 128 mesh nodes of device (b, p - 1), or among the first 128 of device (b, p + 1), patch indices taken modulo 8.
All inputs are finite; a program needn't handle non-finite values.
Results may differ from the reference program's by a relative error of at most 0.023.
Values may be sent and summed in bfloat16 or wider, within the bound.
A program may use at most 128 MiB of HBM per device.

```python
import math
import jax
import jax.numpy as jnp
import numpy as np
from jax import lax

L = 512
CIN = 227
GRID_DEV = 256
MESH_DEV = 256
TOP = 4
DEG = 6
RIM = 128
LAYERS = 2
PEERS = 128
PATCHES = 8
CAP = 16
GRID = 32768
MESH = 32768


def draw_mesh_src(key, part):
    key = jax.random.fold_in(key, 7)
    key_side, key_near, key_edge = jax.random.split(key, 3)
    rows = jnp.arange(MESH, dtype=jnp.int32)
    device = rows // MESH_DEV
    band_of = device // PATCHES
    patch_of = device % PATCHES
    side = jax.random.randint(key_side, (MESH, DEG), -1, 2)
    near = jax.random.randint(key_near, (MESH, DEG), 0, MESH_DEV)
    edge_node = jax.random.randint(key_edge, (MESH, DEG), 0, RIM)
    other = (patch_of[:, None] + side + PATCHES) % PATCHES
    local = jnp.where(side == 0, near, jnp.where(side < 0, MESH_DEV - RIM + edge_node, edge_node))
    return ((band_of[:, None] * PATCHES + other) * MESH_DEV + local).astype(jnp.int32)


def set_ends(entries, key, least, largest):
    place = [jax.random.randint(jax.random.fold_in(key, axis), (), 0, length) for axis, length in enumerate(entries.shape)]
    widest = entries.shape.index(max(entries.shape))
    next_to = place[:widest] + [(place[widest] + 1) % entries.shape[widest]] + place[widest + 1:]
    return entries.at[tuple(place)].set(least).at[tuple(next_to)].set(largest)


def level_of(rng, dims, pieces, smallest, largest):
    def one(dim, parts):
        draws = jax.random.uniform(jax.random.fold_in(jax.random.fold_in(rng, 6), dim), (parts,), jnp.float32, smallest / len(pieces), largest / len(pieces))
        return jnp.repeat(jnp.exp(draws), dims[dim] // parts).reshape((-1,) + (1,) * (len(dims) - dim - 1))

    loudness = one(*pieces[0])
    for cut in pieces[1:]:
        loudness = loudness * one(*cut)
    return loudness


def deal_out(key, own, number, rows, amount, top, limit, lean):
    sequence = jax.random.permutation(key, amount)
    packed, ordinary = load_shares(amount, rows * top, limit, lean, True), load_shares(amount, rows * top, limit, lean, False)
    places = jnp.arange(amount)

    def named(tallies, offset_by):
        used = int((tallies > 0).sum())
        fixed = max(1, used // 4)
        shifted = fixed + (places - fixed + offset_by * (used - fixed)) % max(1, amount - fixed)
        return jnp.zeros((amount,), jnp.int32).at[sequence[jnp.where(places < fixed, places, shifted)]].set(jnp.asarray(tallies, jnp.int32))

    tallies = jnp.where(number % 4 == 0, named(packed, number // 4), named(ordinary, number - number // 4 - 1))
    mixed = jax.random.permutation(jax.random.fold_in(own, 3), amount)
    source_of, receiver = mixed[0:amount // 2 * 2:2], mixed[1:amount // 2 * 2:2]
    room = jnp.minimum(tallies[source_of] - 1, limit - tallies[receiver]) // 2
    room = jnp.where((source_of == sequence[0]) | (receiver == sequence[0]) | (tallies[receiver] == 0), 0, jnp.maximum(room, 0))
    shifted = jax.random.randint(jax.random.fold_in(own, 4), (amount // 2,), 0, 1 << 20) % (room + 1)
    tallies = tallies.at[source_of].add(-shifted).at[receiver].add(shifted)
    members = jnp.searchsorted(jnp.cumsum(tallies), jnp.arange(rows * top), side="right").astype(jnp.int32)
    table = members.reshape(top, rows).T
    table = table[jax.random.permutation(jax.random.fold_in(own, 1), rows)]
    offset_by = jax.random.randint(jax.random.fold_in(own, 2), (rows, 1), 0, top)
    return jnp.take_along_axis(table, (jnp.arange(top)[None, :] + offset_by) % top, axis=1)


def load_shares(amount, total, bound, slope, full):
    weights = [(1 << 20) // math.isqrt(grade ** slope) + 1 for grade in range(1, amount + 1)]
    largest = bound if full else min(bound, max(-(-total // amount), total * weights[0] // sum(weights)))
    least = 1 if total - largest >= amount - 1 else 0
    counts, surplus = [largest] + [least] * (amount - 1), total - largest - least * (amount - 1)
    while surplus > 0:
        free = [i for i in range(1, amount) if counts[i] < largest] or [i for i in range(1, amount) if counts[i] < bound]
        pool, left = sum([weights[i] for i in free]), surplus
        for i in free:
            more = min(bound - counts[i], max(1, left * weights[i] // pool), surplus)
            counts[i] = counts[i] + more
            surplus = surplus - more
    return np.array(counts)


def noise(own_key, extent, spread, reach, shards=(), kind=jnp.bfloat16):
    factor_of = level_of(own_key, extent, shards, -0.22, 0.18) if shards else 1.0
    values = jax.random.normal(own_key, extent, jnp.float32) * spread * factor_of
    return jnp.minimum(jnp.maximum(values, -reach), reach).astype(kind)


def setup_inputs(seed: int = 0) -> dict:
    seeds = jax.random.split(jax.random.key(seed), 14)
    grid_feat = noise(seeds[0], (GRID, CIN), 1.0, 6.0, ((0, 128),))
    mesh_state = noise(seeds[1], (MESH, L), 1.0, 6.0, ((0, 128),))
    g2m_dest_keys = jax.random.split(jax.random.fold_in(seeds[2], 1), GRID // GRID_DEV)
    g2m_dest_turns = jax.random.permutation(jax.random.fold_in(seeds[2], 3), GRID // GRID_DEV)
    g2m_dest = jax.vmap(lambda own, number: deal_out(jax.random.fold_in(seeds[2], 2), own, number, GRID_DEV, PEERS, TOP, CAP, 2))(g2m_dest_keys, g2m_dest_turns).reshape((GRID, TOP))
    g2m_node = set_ends(jax.random.randint(seeds[3], (GRID, TOP), 0, MESH_DEV), jax.random.fold_in(seeds[3], 1), 0, MESH_DEV - 1).astype(jnp.int32)
    g2m_dist = jnp.clip(jnp.exp(math.log(2.0) - 2.0794415 * jax.random.uniform(seeds[4], (GRID, TOP), jnp.float32) ** level_of(seeds[4], (GRID, TOP), ((0, 128),), -0.2, 0.2)), 0.25, 2.0).astype(jnp.bfloat16)
    mesh_src = draw_mesh_src(jax.random.fold_in(seeds[13], 71), 0)
    w_embed = noise(seeds[6], (CIN, L), CIN ** -0.5, 0.375)
    w_send = noise(seeds[7], (L, L), L ** -0.5, 0.25)
    w_recv = noise(seeds[8], (L, L), L ** -0.5, 0.25)
    w_node = noise(seeds[9], (L, L), L ** -0.5, 0.25)
    edge_vec = noise(seeds[10], (L,), 1.0, 4.0)
    proc_weights = noise(seeds[11], (LAYERS, 3, L, L), L ** -0.5, 0.25)
    cotangent = noise(seeds[12], (MESH, L), 1.0, 6.0, ((0, 128),))
    return dict(grid_feat=grid_feat, mesh_state=mesh_state, g2m_dest=g2m_dest, g2m_node=g2m_node, g2m_dist=g2m_dist, mesh_src=mesh_src, w_embed=w_embed, w_send=w_send, w_recv=w_recv, w_node=w_node, edge_vec=edge_vec, proc_weights=proc_weights, cotangent=cotangent)


def dsilu(value):
    sig = jax.nn.sigmoid(value)
    return sig * (1.0 + value * (1.0 - sig))


def dot_tr(left, right):
    return lax.dot_general(left, right, (((1,), (1,)), ((), ())), preferred_element_type=jnp.float32)


def edge_preact(proj_rows, target, dist, recv_proj, edge_vec):
    repeated = jnp.repeat(proj_rows.astype(jnp.float32), TOP, axis=0)
    return repeated + recv_proj[target] + dist.astype(jnp.float32)[:, None] * edge_vec.astype(jnp.float32)[None, :]


def reference(grid_feat, mesh_state, g2m_dest, g2m_node, g2m_dist, mesh_src, w_embed, w_send, w_recv, w_node, edge_vec, proc_weights, cotangent):
    embed_pre = jnp.dot(grid_feat, w_embed, preferred_element_type=jnp.float32)
    grid_latent = jax.nn.silu(embed_pre).astype(jnp.bfloat16)
    sent_proj = jnp.dot(grid_latent, w_send, preferred_element_type=jnp.float32).astype(jnp.bfloat16)
    recv_proj = jnp.dot(mesh_state, w_recv, preferred_element_type=jnp.float32)
    target = (g2m_dest * MESH_DEV + g2m_node).astype(jnp.int32)
    blocks = (sent_proj.reshape(PEERS, GRID_DEV, L), target.reshape(PEERS, GRID_DEV * TOP), g2m_dist.reshape(PEERS, GRID_DEV * TOP))

    def forward_block(total, block):
        proj_rows, tgt, dist = block
        preact = edge_preact(proj_rows, tgt, dist, recv_proj, edge_vec)
        return total.at[tgt].add(jax.nn.silu(preact)), None

    summed, unused = lax.scan(forward_block, jnp.zeros((MESH, L), jnp.float32), blocks)
    aggregate = summed.astype(jnp.bfloat16)
    node_pre = jnp.dot(aggregate, w_node, preferred_element_type=jnp.float32)
    hidden = (mesh_state.astype(jnp.float32) + jax.nn.silu(node_pre)).astype(jnp.bfloat16)
    saved = []
    for layer in range(LAYERS):
        w_s = proc_weights[layer, 0]
        w_r = proc_weights[layer, 1]
        w_a = proc_weights[layer, 2]
        send_p = jnp.dot(hidden, w_s, preferred_element_type=jnp.float32)
        recv_p = jnp.dot(hidden, w_r, preferred_element_type=jnp.float32)
        total = jnp.zeros((MESH, L), jnp.float32)
        for slot in range(DEG):
            total = total + jax.nn.silu(send_p[mesh_src[:, slot]] + recv_p)
        mean_msg = (total / DEG).astype(jnp.bfloat16)
        upd_pre = jnp.dot(mean_msg, w_a, preferred_element_type=jnp.float32)
        saved.append((send_p, recv_p, upd_pre))
        hidden = (hidden.astype(jnp.float32) + jax.nn.silu(upd_pre)).astype(jnp.bfloat16)
    mesh_out = hidden
    grad = cotangent.astype(jnp.float32)
    for layer in reversed(range(LAYERS)):
        w_s = proc_weights[layer, 0]
        w_r = proc_weights[layer, 1]
        w_a = proc_weights[layer, 2]
        send_p, recv_p, upd_pre = saved[layer]
        grad_z = (grad * dsilu(upd_pre)).astype(jnp.bfloat16)
        grad_mean = dot_tr(grad_z, w_a)
        grad_recv = jnp.zeros((MESH, L), jnp.float32)
        grad_send = jnp.zeros((MESH, L), jnp.float32)
        for slot in range(DEG):
            preact = send_p[mesh_src[:, slot]] + recv_p
            grad_pre = (grad_mean / DEG * dsilu(preact)).astype(jnp.bfloat16).astype(jnp.float32)
            grad_recv = grad_recv + grad_pre
            grad_send = grad_send.at[mesh_src[:, slot]].add(grad_pre)
        grad = grad + dot_tr(grad_recv.astype(jnp.bfloat16), w_r) + dot_tr(grad_send.astype(jnp.bfloat16), w_s)
    grad_z0 = (grad * dsilu(node_pre)).astype(jnp.bfloat16)
    grad_agg = dot_tr(grad_z0, w_node)

    def backward_block(total, block):
        proj_rows, tgt, dist = block
        preact = edge_preact(proj_rows, tgt, dist, recv_proj, edge_vec)
        grad_enc = (grad_agg[tgt] * dsilu(preact)).astype(jnp.bfloat16).astype(jnp.float32)
        row_sum = grad_enc.reshape(GRID_DEV, TOP, L).sum(axis=1).astype(jnp.bfloat16)
        return total.at[tgt].add(grad_enc), row_sum

    grad_rproj, grad_sproj = lax.scan(backward_block, jnp.zeros((MESH, L), jnp.float32), blocks)
    mesh_grad = (grad + dot_tr(grad_rproj.astype(jnp.bfloat16), w_recv)).astype(jnp.bfloat16)
    grad_latent = dot_tr(grad_sproj.reshape(GRID, L), w_send)
    grad_embed = (grad_latent * dsilu(embed_pre)).astype(jnp.bfloat16)
    grid_grad = dot_tr(grad_embed, w_embed).astype(jnp.bfloat16)
    return mesh_out, mesh_grad, grid_grad
```

```python
import jax
import jax.numpy as jnp
from jax import lax
from jax.sharding import PartitionSpec as P

TOP = 4
DEG = 6
RIM = 128
LAYERS = 2
CAP = 16
WIDE = 256
AXES = ("band", "patch")
F32 = jnp.float32
BF16 = jnp.bfloat16


def mm(left, right):
    return lax.dot_general(left, right, (((1,), (0,)), ((), ())), preferred_element_type=F32)


def mm_t(left, right):
    return lax.dot_general(left, right, (((1,), (1,)), ((), ())), preferred_element_type=F32)


def t_mm(left, right):
    return lax.dot_general(left, right, (((0,), (0,)), ((), ())), preferred_element_type=F32)


def act(value):
    sig = jax.nn.sigmoid(value)
    out = value * sig
    return out, sig + out * (1.0 - sig)


def shift(x, up):
    n = lax.axis_size("patch")
    return lax.ppermute(x, "patch", [(i, (i + (1 if up else -1)) % n) for i in range(n)])


def exchange(x):
    return lax.all_to_all(x, AXES, split_axis=0, concat_axis=0, tiled=True)


def local(grid_feat, mesh_state, g2m_dest, g2m_node, g2m_dist, mesh_src, w_embed, w_send, w_recv, w_node, edge_vec, proc_weights, cotangent):
    peers = lax.axis_size(AXES)
    patches = lax.axis_size("patch")
    rows, cin = grid_feat.shape
    nodes, width = mesh_state.shape
    slots = peers * CAP
    own = lax.axis_index(AXES)
    dest_t, node_t, dist_t = g2m_dest.T, g2m_node.T, g2m_dist.T

    peer_ids = jnp.arange(peers, dtype=jnp.int32)[:, None]
    named = sum([(dest_t[k][None, :] == peer_ids).astype(BF16) for k in range(TOP)])
    before = (jnp.arange(rows)[:, None] < jnp.arange(rows)[None, :]).astype(BF16)
    rank = mm(named, before)
    place = jnp.where(named > 0, rank, -1.0)
    pick = (
        (place[:, None, :] == jnp.arange(CAP, dtype=F32)[None, :, None]).astype(BF16).reshape(slots, rows)
    )
    spare = WIDE - cin - 3 * TOP
    packed = jnp.concatenate(
        [grid_feat, (g2m_dest + 1).astype(BF16), (g2m_node + 1).astype(BF16), g2m_dist, jnp.zeros((rows, spare), BF16)],
        axis=1,
    )
    sent = mm(pick, packed).astype(BF16)
    got = exchange(sent.reshape(peers, CAP, WIDE)).reshape(slots, WIDE)

    dest = got[:, cin : cin + TOP].astype(F32)
    mine = dest == (own + 1).astype(F32)
    node = jnp.sum(jnp.where(mine, got[:, cin + TOP : cin + 2 * TOP].astype(F32), 0.0), axis=1, keepdims=True)
    dist = jnp.sum(jnp.where(mine, got[:, cin + 2 * TOP : cin + 3 * TOP].astype(F32), 0.0), axis=1, keepdims=True)
    here = (node == jnp.arange(1, nodes + 1, dtype=F32)[None, :]).astype(BF16)
    w_embed_wide = jnp.concatenate([w_embed, jnp.zeros((WIDE - cin, width), BF16)], axis=0)

    latent, d_embed = act(mm(got, w_embed_wide))
    recv_proj = mm(mesh_state, w_recv).astype(BF16)
    enc_pre = mm(latent.astype(BF16), w_send) + mm(here, recv_proj) + dist * edge_vec.astype(F32)[None, :]
    enc, d_enc = act(enc_pre)
    aggregate = t_mm(here, enc.astype(BF16)).astype(BF16)
    upd, d_node = act(mm(aggregate, w_node))
    hidden = (mesh_state.astype(F32) + upd).astype(BF16)

    own_patch = own % patches
    src_dev = mesh_src // nodes
    src_local = mesh_src % nodes
    left_side = src_dev % patches == (own_patch + patches - 1) % patches
    ext_index = jnp.where(
        src_dev == own,
        RIM + src_local,
        jnp.where(left_side, src_local - (nodes - RIM), RIM + nodes + src_local),
    )
    wide = nodes + 2 * RIM
    chosen = (ext_index.T.reshape(-1)[:, None] == jnp.arange(wide)[None, :]).astype(BF16)
    saved = []
    for layer in range(LAYERS):
        w_s, w_r, w_a = [proc_weights[layer, i] for i in range(3)]
        ext = jnp.concatenate([shift(hidden[nodes - RIM :], True), hidden, shift(hidden[:RIM], False)], axis=0)
        send_p = mm(ext, w_s).astype(BF16)
        recv_p = mm(hidden, w_r)
        proc, d_proc = act(mm(chosen, send_p).reshape(DEG, nodes, width) + recv_p[None])
        mean_msg = (proc.sum(axis=0) / DEG).astype(BF16)
        upd, d_upd = act(mm(mean_msg, w_a))
        saved.append((d_proc, d_upd))
        hidden = (hidden.astype(F32) + upd).astype(BF16)
    grad = cotangent.astype(F32)
    for layer in reversed(range(LAYERS)):
        w_s, w_r, w_a = [proc_weights[layer, i] for i in range(3)]
        d_proc, d_upd = saved[layer]
        grad_mean = mm_t((grad * d_upd).astype(BF16), w_a) / DEG
        grad_pre = (grad_mean[None] * d_proc).astype(BF16)
        grad_recv = grad_pre.astype(F32).sum(axis=0).astype(BF16)
        grad_ext = t_mm(chosen, grad_pre.reshape(DEG * nodes, width))
        from_right = shift(grad_ext[:RIM].astype(BF16), False)
        from_left = shift(grad_ext[RIM + nodes :].astype(BF16), True)
        grad_send = grad_ext[RIM : RIM + nodes]
        grad_send = grad_send.at[:RIM].add(from_left.astype(F32)).at[nodes - RIM :].add(from_right.astype(F32))
        grad = grad + mm_t(grad_recv, w_r) + mm_t(grad_send.astype(BF16), w_s)
    grad_agg = mm_t((grad * d_node).astype(BF16), w_node).astype(BF16)
    grad_enc = (mm(here, grad_agg) * d_enc).astype(BF16)
    grad_rproj = t_mm(here, grad_enc).astype(BF16)
    mesh_grad = (grad + mm_t(grad_rproj, w_recv)).astype(BF16)
    grad_embed = (mm_t(grad_enc, w_send) * d_embed).astype(BF16)
    back = exchange(mm_t(grad_embed, w_embed_wide).astype(BF16).reshape(peers, CAP, WIDE)).reshape(slots, WIDE)
    grid_grad = t_mm(pick, back)[:, :cin].astype(BF16)
    return hidden, mesh_grad, grid_grad


def solution(mesh):
    split = P(AXES, None)
    return jax.shard_map(
        local,
        mesh=mesh,
        in_specs=(split,) * 6 + (P(),) * 6 + (split,),
        out_specs=(split,) * 3,
        check_vma=False,
    )
```

```python
import functools

import jax
import jax.numpy as jnp
from jax import lax
from jax.experimental import pallas as pl
from jax.experimental.pallas import tpu as pltpu
from jax.sharding import PartitionSpec as P

TOP = 4
DEG = 6
RIM = 128
LAYERS = 2
CAP = 16
WIDE = 256
META = 240
AXES = ("band", "patch")
F32 = jnp.float32
BF16 = jnp.bfloat16
I32 = jnp.int32
GROUP = 16
ROWS = GROUP * CAP


def mm(left, right):
    return lax.dot_general(left, right, (((1,), (0,)), ((), ())), preferred_element_type=F32)


def mm_t(left, right):
    return lax.dot_general(left, right, (((1,), (1,)), ((), ())), preferred_element_type=F32)


def act(value):
    sig = 0.5 * jnp.tanh(0.5 * value) + 0.5
    out = value * sig
    return out, sig + out * (1.0 - sig)


def iota(shape, dim):
    return lax.broadcasted_iota(I32, shape, dim)


def onehot(mask):
    return jnp.where(mask, 1.0, 0.0).astype(BF16)


def offsets(slot):
    dp = slot % 8
    return (slot // 8 + 5 * dp) % 16, dp


def kernel(
    feat_t, dest_t, node_t, dist_t, src_t, w_embed, edge_vec,
    state_hbm, w_send_hbm, w_recv_hbm, w_node_hbm, proc_hbm, cot_hbm,
    mesh_out, mesh_grad, grid_grad_t,
    state, w_send, w_recv, w_node, proc, cot, w_emb,
    w_send_t, w_recv_t, w_node_t, proc_t, w_emb_t,
    meta, packed_t, packed, place, send_buf, recv_buf, back_buf, ret_buf, unpick,
    recv_proj, here, here_t, d_emb, d_enc, acc, d_node,
    chosen, chosen_t, pre, d_proc, d_upd, hid, send_p, grad_pre, grad_ext, grad, rims,
    load_sem, fwd_send, fwd_recv, bwd_send, bwd_recv, rim_send, rim_recv, entered,
):
    bands, patches = lax.axis_size("band"), lax.axis_size("patch")
    peers = bands * patches
    groups = peers // GROUP
    nodes, width = state.shape
    cin, rows = feat_t.shape
    b, p = lax.axis_index("band"), lax.axis_index("patch")
    left, right = (p + patches - 1) % patches, (p + 1) % patches

    loads = [
        pltpu.make_async_copy(src, dst, load_sem.at[i])
        for i, (src, dst) in enumerate(
            [(state_hbm, state), (w_recv_hbm, w_recv), (w_send_hbm, w_send), (w_node_hbm, w_node), (proc_hbm, proc), (cot_hbm, cot)]
        )
    ]
    for load in loads:
        load.start()

    barrier = pltpu.get_barrier_semaphore()

    def greet_patch(i, carry):
        pl.semaphore_signal(barrier, inc=1, device_id=(b, (p + i) % patches), device_id_type=pl.DeviceIdType.MESH)
        return carry

    def greet_band(i, carry):
        pl.semaphore_signal(barrier, inc=1, device_id=((b + i) % bands, p), device_id_type=pl.DeviceIdType.MESH)
        return carry

    lax.fori_loop(1, patches, greet_patch, 0)
    lax.fori_loop(1, bands, greet_band, 0)

    meta[...] = jnp.zeros_like(meta)
    dest = dest_t[...]
    meta[0:TOP, :] = (dest + 1).astype(F32)
    meta[TOP : 2 * TOP, :] = (node_t[...] + 1).astype(F32)
    meta[2 * TOP : 3 * TOP, :] = dist_t[...].astype(F32)
    packed_t[...] = jnp.zeros_like(packed_t)
    packed_t[0:cin, :] = feat_t[...]
    packed_t[META:WIDE, :] = meta[...].astype(BF16)
    packed[...] = packed_t[...].T
    slot = iota((peers, rows), 0)
    slot_p = slot & (patches - 1)
    slot_b = (lax.shift_right_logical(slot, 3) + 5 * slot_p) & (bands - 1)
    slot_id = ((slot_b + b) & (bands - 1)) * patches + ((slot_p + p) & (patches - 1))
    named = jnp.zeros((peers, rows), F32)
    for k in range(TOP):
        named = named + jnp.where(dest[k : k + 1, :] == slot_id, 1.0, 0.0)
    before = onehot(iota((rows, rows), 0) < iota((rows, rows), 1))
    rank = mm(named.astype(BF16), before)
    place[...] = jnp.where(named > 0.5, rank, -1.0).astype(BF16)

    def pick_group(g):
        spread = onehot(lax.shift_right_logical(iota((ROWS, peers), 0) + g * ROWS, 4) == iota((ROWS, peers), 1))
        slot_place = mm(spread, place[...])
        return onehot(slot_place == (iota((ROWS, rows), 0) & (CAP - 1)).astype(F32))

    def fill(g, carry):
        send_buf[pl.ds(pl.multiple_of(g * ROWS, ROWS), ROWS), :] = mm(pick_group(g), packed[...]).astype(BF16)
        return carry

    lax.fori_loop(0, groups, fill, 0)

    pl.semaphore_wait(barrier, patches + bands - 2)

    def greet_again(i, carry):
        pl.semaphore_signal(entered, inc=1, device_id=((b + i) % bands, p), device_id_type=pl.DeviceIdType.MESH)
        return carry

    lax.fori_loop(1, bands, greet_again, 0)
    pl.semaphore_wait(entered, bands - 1)

    def block(t):
        return pl.ds(pl.multiple_of(t * CAP, CAP), CAP)

    def send_fwd(t, carry):
        db, dp = offsets(t)
        pltpu.make_async_remote_copy(
            send_buf.at[block(t), :], recv_buf.at[block(t), :], fwd_send, fwd_recv.at[t // GROUP],
            device_id=((b + db) % bands, (p + dp) % patches), device_id_type=pl.DeviceIdType.MESH,
        ).start()
        return carry

    def send_bwd(t, carry):
        db, dp = offsets(t)
        pltpu.make_async_remote_copy(
            back_buf.at[block(t), :], ret_buf.at[block(t), :], bwd_send, bwd_recv.at[t // GROUP],
            device_id=((b + bands - db) % bands, (p + patches - dp) % patches), device_id_type=pl.DeviceIdType.MESH,
        ).start()
        return carry

    pltpu.make_async_copy(send_buf.at[pl.ds(0, CAP), :], recv_buf.at[pl.ds(0, CAP), :], fwd_recv.at[0]).start()
    lax.fori_loop(1, peers, send_fwd, 0)

    w_emb[...] = jnp.zeros_like(w_emb)
    w_emb[0:cin, :] = w_embed[...]
    w_emb_t[...] = w_emb[...].T
    loads[0].wait()
    loads[1].wait()
    recv_proj[...] = mm(state[...], w_recv[...]).astype(BF16)
    w_recv_t[...] = w_recv[...].T
    loads[2].wait()
    w_send_t[...] = w_send[...].T
    loads[3].wait()
    w_node_t[...] = w_node[...].T
    loads[4].wait()
    for layer in range(LAYERS):
        for i in range(3):
            proc_t[layer, i] = proc[layer, i].T
    loads[5].wait()
    unit = onehot(iota((ROWS, ROWS), 0) == iota((ROWS, ROWS), 1))
    src = src_t[...]
    here_first = (b * patches + p) * nodes
    left_first = (b * patches + left) * nodes
    right_first = (b * patches + right) * nodes
    for k in range(DEG):
        row = src[k : k + 1, :]
        own_row = jnp.where((row >= here_first) & (row < here_first + nodes), row - here_first, -1)
        rim_row = jnp.where(
            (row >= left_first + nodes - RIM) & (row < left_first + nodes),
            row - left_first - (nodes - RIM),
            jnp.where((row >= right_first) & (row < right_first + RIM), row - right_first + RIM, -1),
        )
        e = iota((nodes, nodes), 0)
        own_t = onehot(own_row == e)
        rim_t = onehot(rim_row == e)
        cols = slice(k * nodes, (k + 1) * nodes)
        chosen_t[0:nodes, cols] = own_t
        chosen_t[nodes : 2 * nodes, cols] = rim_t
        chosen[cols, 0:nodes] = mm_t(unit, own_t).astype(BF16)
        chosen[cols, nodes : 2 * nodes] = mm_t(unit, rim_t).astype(BF16)

    def fill_unpick(g, carry):
        unpick[g] = mm_t(unit, pick_group(g)).astype(BF16)
        return carry

    lax.fori_loop(0, groups, fill_unpick, 0)

    me1 = (b * patches + p + 1).astype(F32)
    c0 = META - 128
    sel_c, sel_l = iota((128, 384), 0), iota((128, 384), 1)
    sel_k = sel_l & 127
    select = onehot((sel_k < TOP) & (sel_c == c0 + sel_k + TOP * lax.shift_right_logical(sel_l, 7)))
    select_t = onehot(iota((16, 128), 1) == c0 + iota((16, 128), 0))
    ones = jnp.ones((128, nodes), BF16)
    edges = jnp.broadcast_to(edge_vec[...].astype(F32), (128, width)).astype(BF16)
    acc[...] = jnp.zeros_like(acc)

    def encode(g, carry):
        at = pl.ds(pl.multiple_of(g * ROWS, ROWS), ROWS)
        pltpu.make_async_copy(recv_buf.at[at, :], recv_buf.at[at, :], fwd_recv.at[g]).wait()
        got = recv_buf[at, :]
        tail = got[:, 128:256]
        fields = mm(tail, select)
        mine = fields[:, 0:128] == me1
        node = mm(jnp.where(mine, fields[:, 128:256], 0.0).astype(BF16), ones)
        length = mm(jnp.where(mine, fields[:, 256:384], 0.0).astype(BF16), edges)
        at_node = onehot(node == (iota((ROWS, nodes), 1) + 1).astype(F32))
        here[at, :] = at_node
        fields_t = mm_t(select_t, tail)
        node_row = jnp.zeros((1, ROWS), F32)
        for k in range(TOP):
            node_row = node_row + jnp.where(fields_t[k : k + 1, :] == me1, fields_t[TOP + k : TOP + k + 1, :], 0.0)
        at_node_t = onehot(node_row == (iota((nodes, ROWS), 0) + 1).astype(F32))
        here_t[g] = at_node_t
        latent, slope = act(mm(got, w_emb[...]))
        d_emb[at, :] = slope.astype(BF16)
        enc, slope = act(mm(latent.astype(BF16), w_send[...]) + mm(at_node, recv_proj[...]) + length)
        d_enc[at, :] = slope.astype(BF16)
        acc[...] += mm(at_node_t, enc.astype(BF16))
        return carry

    lax.fori_loop(0, groups, encode, 0)

    upd, slope = act(mm(acc[...].astype(BF16), w_node[...]))
    d_node[...] = slope
    hid[0] = (state[...].astype(F32) + upd).astype(BF16)

    def swap_rims(step, to_left, to_right):
        one = pltpu.make_async_remote_copy(
            to_left, rims.at[step, 1], rim_send.at[step, 0], rim_recv.at[step, 1],
            device_id=(b, left), device_id_type=pl.DeviceIdType.MESH,
        )
        two = pltpu.make_async_remote_copy(
            to_right, rims.at[step, 0], rim_send.at[step, 1], rim_recv.at[step, 0],
            device_id=(b, right), device_id_type=pl.DeviceIdType.MESH,
        )
        one.start()
        two.start()
        return one, two

    swaps = []
    for layer in range(LAYERS):
        one, two = swap_rims(layer, hid.at[layer, pl.ds(0, RIM), :], hid.at[layer, pl.ds(nodes - RIM, RIM), :])
        swaps += [one, two]
        now = hid[layer]
        recv_p = mm(now, proc[layer, 1])
        send_p[0:nodes, :] = mm(now, proc[layer, 0]).astype(BF16)
        one.wait_recv()
        two.wait_recv()
        send_p[nodes : nodes + RIM, :] = mm(rims[layer, 0], proc[layer, 0]).astype(BF16)
        send_p[nodes + RIM : nodes + 2 * RIM, :] = mm(rims[layer, 1], proc[layer, 0]).astype(BF16)
        for k in range(DEG):
            at = slice(k * nodes, (k + 1) * nodes)
            out, slope = act(recv_p + mm(chosen[at, :], send_p[...]))
            d_proc[layer, at, :] = slope.astype(BF16)
            acc[...] = out if k == 0 else acc[...] + out
        upd, slope = act(mm((acc[...] * (1.0 / DEG)).astype(BF16), proc[layer, 2]))
        d_upd[layer] = slope
        after = (now.astype(F32) + upd).astype(BF16)
        if layer + 1 < LAYERS:
            hid[layer + 1] = after
        else:
            mesh_out[...] = after

    grad[...] = cot[...].astype(F32)
    for layer in reversed(range(LAYERS)):
        mean = mm((grad[...] * d_upd[layer]).astype(BF16), proc_t[layer, 2]) * (1.0 / DEG)
        for k in range(DEG):
            at = slice(k * nodes, (k + 1) * nodes)
            part = mean * d_proc[layer, at, :].astype(F32)
            grad_pre[at, :] = part.astype(BF16)
            acc[...] = part if k == 0 else acc[...] + part
        grad_ext[layer] = mm(chosen_t[nodes : 2 * nodes, :], grad_pre[...]).astype(BF16)
        one, two = swap_rims(LAYERS + layer, grad_ext.at[layer, pl.ds(0, RIM), :], grad_ext.at[layer, pl.ds(RIM, RIM), :])
        swaps += [one, two]
        own = mm(chosen_t[0:nodes, :], grad_pre[...])
        grad[...] += mm(acc[...].astype(BF16), proc_t[layer, 1])
        one.wait_recv()
        two.wait_recv()
        rim = jnp.concatenate([rims[LAYERS + layer, 0], rims[LAYERS + layer, 1]], axis=0)
        grad[...] += mm((own + rim.astype(F32)).astype(BF16), proc_t[layer, 0])

    agg = mm((grad[...] * d_node[...]).astype(BF16), w_node_t[...]).astype(BF16)
    recv_proj[...] = agg

    def decode(g, carry):
        at = pl.ds(pl.multiple_of(g * ROWS, ROWS), ROWS)
        edge = (mm(here[at, :], recv_proj[...]) * d_enc[at, :].astype(F32)).astype(BF16)
        d_enc[at, :] = edge
        emb = (mm(edge, w_send_t[...]) * d_emb[at, :].astype(F32)).astype(BF16)
        back_buf[at, :] = mm(emb, w_emb_t[...]).astype(BF16)
        lax.fori_loop(jnp.maximum(g * GROUP, 1), (g + 1) * GROUP, send_bwd, 0)
        return carry

    lax.fori_loop(0, groups, decode, 0)
    pltpu.make_async_copy(back_buf.at[pl.ds(0, CAP), :], ret_buf.at[pl.ds(0, CAP), :], bwd_recv.at[0]).start()
    acc[...] = jnp.zeros_like(acc)

    def scatter(g, carry):
        at = pl.ds(pl.multiple_of(g * ROWS, ROWS), ROWS)
        acc[...] += mm(here_t[g], d_enc[at, :])
        return carry

    lax.fori_loop(0, groups, scatter, 0)
    mesh_grad[...] = (grad[...] + mm(acc[...].astype(BF16), w_recv_t[...])).astype(BF16)

    acc[...] = jnp.zeros_like(acc)

    def collect(g, carry):
        at = pl.ds(pl.multiple_of(g * ROWS, ROWS), ROWS)
        pltpu.make_async_copy(ret_buf.at[at, :], ret_buf.at[at, :], bwd_recv.at[g]).wait()
        acc[:, 0:WIDE] += mm(unpick[g], ret_buf[at, :])
        return carry

    lax.fori_loop(0, groups, collect, 0)
    packed_t[...] = mm_t(unit, acc[:, 0:WIDE].astype(BF16)).astype(BF16)
    grid_grad_t[...] = packed_t[0:cin, :]

    for swap in swaps:
        swap.wait_send()
    others = pl.ds(CAP, (peers - 1) * CAP)
    pltpu.make_async_copy(send_buf.at[others, :], send_buf.at[others, :], fwd_send).wait()
    pltpu.make_async_copy(back_buf.at[others, :], back_buf.at[others, :], bwd_send).wait()


def local(grid_feat, mesh_state, g2m_dest, g2m_node, g2m_dist, mesh_src, w_embed, w_send, w_recv, w_node, edge_vec, proc_weights, cotangent):
    peers = lax.axis_size(AXES)
    rows, cin = grid_feat.shape
    nodes, width = mesh_state.shape
    slots = peers * CAP
    groups = peers // GROUP
    vmem = pl.BlockSpec(memory_space=pltpu.VMEM)
    anywhere = pl.BlockSpec(memory_space=pl.ANY)
    square = pltpu.VMEM((width, width), BF16)
    stack = pltpu.VMEM((LAYERS, 3, width, width), BF16)
    tile = pltpu.VMEM((nodes, width), BF16)
    mesh_out, mesh_grad, grid_grad_t = pl.pallas_call(
        kernel,
        out_shape=(
            jax.ShapeDtypeStruct((nodes, width), BF16),
            jax.ShapeDtypeStruct((nodes, width), BF16),
            jax.ShapeDtypeStruct((cin, rows), BF16),
        ),
        in_specs=[vmem] * 7 + [anywhere] * 6,
        out_specs=(vmem,) * 3,
        scratch_shapes=[
            tile, square, square, square, stack, tile, pltpu.VMEM((WIDE, width), BF16),
            square, square, square, stack, pltpu.VMEM((width, WIDE), BF16),
            pltpu.VMEM((16, rows), F32), pltpu.VMEM((WIDE, rows), BF16), pltpu.VMEM((rows, WIDE), BF16),
            pltpu.VMEM((peers, rows), BF16),
            pltpu.VMEM((slots, WIDE), BF16), pltpu.VMEM((slots, WIDE), BF16),
            pltpu.VMEM((slots, WIDE), BF16), pltpu.VMEM((slots, WIDE), BF16),
            pltpu.VMEM((groups, rows, ROWS), BF16),
            tile, pltpu.VMEM((slots, nodes), BF16), pltpu.VMEM((groups, nodes, ROWS), BF16),
            pltpu.VMEM((slots, width), BF16), pltpu.VMEM((slots, width), BF16),
            pltpu.VMEM((nodes, width), F32), pltpu.VMEM((nodes, width), F32),
            pltpu.VMEM((DEG * nodes, 2 * nodes), BF16), pltpu.VMEM((2 * nodes, DEG * nodes), BF16),
            pltpu.VMEM((DEG * nodes, width), F32),
            pltpu.VMEM((LAYERS, DEG * nodes, width), BF16), pltpu.VMEM((LAYERS, nodes, width), F32),
            pltpu.VMEM((LAYERS, nodes, width), BF16), pltpu.VMEM((2 * nodes, width), BF16),
            pltpu.VMEM((DEG * nodes, width), BF16), pltpu.VMEM((LAYERS, 2 * RIM, width), BF16),
            pltpu.VMEM((nodes, width), F32), pltpu.VMEM((2 * LAYERS, 2, RIM, width), BF16),
            pltpu.SemaphoreType.DMA((6,)),
            pltpu.SemaphoreType.DMA, pltpu.SemaphoreType.DMA((groups,)),
            pltpu.SemaphoreType.DMA, pltpu.SemaphoreType.DMA((groups,)),
            pltpu.SemaphoreType.DMA((2 * LAYERS, 2)), pltpu.SemaphoreType.DMA((2 * LAYERS, 2)),
            pltpu.SemaphoreType.REGULAR,
        ],
        compiler_params=pltpu.CompilerParams(
            collective_id=0, has_side_effects=True, vmem_limit_bytes=56 * 2**20
        ),
    )(
        grid_feat.T, g2m_dest.T, g2m_node.T, g2m_dist.T, mesh_src.T, w_embed, edge_vec.reshape(1, width),
        mesh_state, w_send, w_recv, w_node, proc_weights, cotangent,
    )
    return mesh_out, mesh_grad, grid_grad_t.T


def solution(mesh):
    split = P(AXES, None)
    return jax.shard_map(
        local,
        mesh=mesh,
        in_specs=(split,) * 6 + (P(),) * 6 + (split,),
        out_specs=(split,) * 3,
        check_vma=False,
    )
```

```python
import functools

import jax
import jax.numpy as jnp
from jax import lax
from jax.experimental import pallas as pl
from jax.experimental.pallas import tpu as pltpu
from jax.sharding import PartitionSpec as P

TOP = 4
DEG = 6
RIM = 128
LAYERS = 2
CAP = 16
WIDE = 256
META = 240
AXES = ("band", "patch")
F32 = jnp.float32
BF16 = jnp.bfloat16
I32 = jnp.int32
GROUP = 16
ROWS = GROUP * CAP


def mm(left, right):
    return lax.dot_general(left, right, (((1,), (0,)), ((), ())), preferred_element_type=F32)


def mm_t(left, right):
    return lax.dot_general(left, right, (((1,), (1,)), ((), ())), preferred_element_type=F32)


def act(value):
    sig = 0.5 * jnp.tanh(0.5 * value) + 0.5
    out = value * sig
    return out, sig + out * (1.0 - sig)


def iota(shape, dim):
    return lax.broadcasted_iota(I32, shape, dim)


def onehot(mask):
    return jnp.where(mask, 1.0, 0.0).astype(BF16)


def wrap(value, size):
    value = jnp.where(value >= 2 * size, value - 2 * size, value)
    return jnp.where(value >= size, value - size, value)


def kernel(
    feat_t, dest_t, node_t, dist_t, src_t, w_embed, edge_vec,
    state_hbm, w_send_hbm, w_recv_hbm, w_node_hbm, proc_hbm, cot_hbm,
    mesh_out, mesh_grad, grid_grad_t,
    state, w_send, w_recv, w_node, proc, cot, w_emb,
    w_send_t, w_recv_t, w_node_t, proc_t, w_emb_t,
    meta, packed_t, packed, place, send_buf, recv_buf, back_buf, ret_buf, unpick,
    recv_proj, here, here_t, d_emb, d_enc, acc, d_node,
    chosen, chosen_t, pre, d_proc, d_upd, hid, send_p, grad_pre, grad_ext, grad, rims,
    load_sem, fwd_send, fwd_recv, bwd_send, bwd_recv, rim_send, rim_recv, entered,
):
    bands, patches = lax.axis_size("band"), lax.axis_size("patch")
    peers = bands * patches
    groups = peers // GROUP
    nodes, width = state.shape
    cin, rows = feat_t.shape
    b, p = lax.axis_index("band"), lax.axis_index("patch")
    left, right = wrap(p + patches - 1, patches), wrap(p + 1, patches)

    loads = [
        pltpu.make_async_copy(src, dst, load_sem.at[i])
        for i, (src, dst) in enumerate(
            [(state_hbm, state), (w_recv_hbm, w_recv), (w_send_hbm, w_send), (w_node_hbm, w_node), (proc_hbm, proc), (cot_hbm, cot)]
        )
    ]
    for load in loads:
        load.start()

    barrier = pltpu.get_barrier_semaphore()

    for i in range(1, bands):
        pl.semaphore_signal(barrier, inc=1, device_id=(wrap(b + i, bands), p), device_id_type=pl.DeviceIdType.MESH)
    for i in range(1, patches):
        pl.semaphore_signal(barrier, inc=1, device_id=(b, wrap(p + i, patches)), device_id_type=pl.DeviceIdType.MESH)

    meta[...] = jnp.zeros_like(meta)
    dest = dest_t[...]
    meta[0:TOP, :] = (dest + 1).astype(F32)
    meta[TOP : 2 * TOP, :] = (node_t[...] + 1).astype(F32)
    meta[2 * TOP : 3 * TOP, :] = dist_t[...].astype(F32)
    packed_t[...] = jnp.zeros_like(packed_t)
    packed_t[0:cin, :] = feat_t[...]
    packed_t[META:WIDE, :] = meta[...].astype(BF16)
    packed[...] = packed_t[...].T
    slot = iota((peers, rows), 0)
    slot_p = slot & (patches - 1)
    slot_b = (lax.shift_right_logical(slot, 3) + 5 * slot_p) & (bands - 1)
    slot_id = ((slot_b + b) & (bands - 1)) * patches + ((slot_p + p) & (patches - 1))
    named = jnp.zeros((peers, rows), F32)
    for k in range(TOP):
        named = named + jnp.where(dest[k : k + 1, :] == slot_id, 1.0, 0.0)
    before = onehot(iota((rows, rows), 0) < iota((rows, rows), 1))
    rank = mm(named.astype(BF16), before)
    place[...] = jnp.where(named > 0.5, rank, -1.0).astype(BF16)

    def pick_group(g):
        spread = onehot(lax.shift_right_logical(iota((ROWS, peers), 0) + g * ROWS, 4) == iota((ROWS, peers), 1))
        slot_place = mm(spread, place[...])
        return onehot(slot_place == (iota((ROWS, rows), 0) & (CAP - 1)).astype(F32))

    def fill(g, carry):
        send_buf[pl.ds(pl.multiple_of(g * ROWS, ROWS), ROWS), :] = mm(pick_group(g), packed[...]).astype(BF16)
        return carry

    lax.fori_loop(0, groups // 2, fill, 0)
    pl.semaphore_wait(barrier, patches + bands - 2)
    for i in range(1, bands):
        pl.semaphore_signal(entered, inc=1, device_id=(wrap(b + i, bands), p), device_id_type=pl.DeviceIdType.MESH)
    lax.fori_loop(groups // 2, groups, fill, 0)
    pl.semaphore_wait(entered, bands - 1)

    def send_group(g, forward, first):
        source, target = (send_buf, recv_buf) if forward else (back_buf, ret_buf)
        sent, received = (fwd_send, fwd_recv) if forward else (bwd_send, bwd_recv)
        for u in range(first, GROUP):
            dp = u % patches
            db = 2 * g + (u // patches + 5 * dp) % bands
            if forward:
                device = (wrap(b + db, bands), wrap(p + dp, patches))
            else:
                device = (wrap(b + 3 * bands - db, bands), wrap(p + patches - dp, patches))
            rows_at = pl.ds(pl.multiple_of(g * ROWS + u * CAP, CAP), CAP)
            pltpu.make_async_remote_copy(
                source.at[rows_at, :], target.at[rows_at, :], sent, received.at[g],
                device_id=device, device_id_type=pl.DeviceIdType.MESH,
            ).start()

    def send_more(g, carry):
        send_group(g, True, 0)
        return carry

    send_group(0, True, 1)
    pltpu.make_async_copy(send_buf.at[pl.ds(0, CAP), :], recv_buf.at[pl.ds(0, CAP), :], fwd_recv.at[0]).start()
    lax.fori_loop(1, groups, send_more, 0)

    w_emb[...] = jnp.zeros_like(w_emb)
    w_emb[0:cin, :] = w_embed[...]
    w_emb_t[...] = w_emb[...].T
    loads[0].wait()
    loads[1].wait()
    recv_proj[...] = mm(state[...], w_recv[...]).astype(BF16)
    w_recv_t[...] = w_recv[...].T
    loads[2].wait()
    w_send_t[...] = w_send[...].T
    loads[3].wait()
    w_node_t[...] = w_node[...].T
    loads[4].wait()
    for layer in range(LAYERS):
        for i in range(3):
            proc_t[layer, i] = proc[layer, i].T
    loads[5].wait()
    unit = onehot(iota((ROWS, ROWS), 0) == iota((ROWS, ROWS), 1))
    src = src_t[...]
    here_first = (b * patches + p) * nodes
    left_first = (b * patches + left) * nodes
    right_first = (b * patches + right) * nodes
    for k in range(DEG):
        row = src[k : k + 1, :]
        own_row = jnp.where((row >= here_first) & (row < here_first + nodes), row - here_first, -1)
        rim_row = jnp.where(
            (row >= left_first + nodes - RIM) & (row < left_first + nodes),
            row - left_first - (nodes - RIM),
            jnp.where((row >= right_first) & (row < right_first + RIM), row - right_first + RIM, -1),
        )
        e = iota((nodes, nodes), 0)
        own_t = onehot(own_row == e)
        rim_t = onehot(rim_row == e)
        cols = slice(k * nodes, (k + 1) * nodes)
        chosen_t[0:nodes, cols] = own_t
        chosen_t[nodes : 2 * nodes, cols] = rim_t
        chosen[cols, 0:nodes] = mm_t(unit, own_t).astype(BF16)
        chosen[cols, nodes : 2 * nodes] = mm_t(unit, rim_t).astype(BF16)

    def fill_unpick(g, carry):
        unpick[g] = mm_t(unit, pick_group(g)).astype(BF16)
        return carry

    lax.fori_loop(0, groups, fill_unpick, 0)

    me1 = (b * patches + p + 1).astype(F32)
    c0 = META - 128
    sel_c, sel_l = iota((128, 384), 0), iota((128, 384), 1)
    sel_k = sel_l & 127
    select = onehot((sel_k < TOP) & (sel_c == c0 + sel_k + TOP * lax.shift_right_logical(sel_l, 7)))
    select_t = onehot(iota((16, 128), 1) == c0 + iota((16, 128), 0))
    ones = jnp.ones((128, nodes), BF16)
    edges = jnp.broadcast_to(edge_vec[...].astype(F32)[None, :], (128, width)).astype(BF16)
    acc[...] = jnp.zeros_like(acc)

    def encode(g, carry):
        at = pl.ds(pl.multiple_of(g * ROWS, ROWS), ROWS)
        pltpu.make_async_copy(recv_buf.at[at, :], recv_buf.at[at, :], fwd_recv.at[g]).wait()
        got = recv_buf[at, :]
        tail = got[:, 128:256]
        fields = mm(tail, select)
        mine = fields[:, 0:128] == me1
        node = mm(jnp.where(mine, fields[:, 128:256], 0.0).astype(BF16), ones)
        length = mm(jnp.where(mine, fields[:, 256:384], 0.0).astype(BF16), edges)
        at_node = onehot(node == (iota((ROWS, nodes), 1) + 1).astype(F32))
        here[at, :] = at_node
        fields_t = mm_t(select_t, tail)
        node_row = jnp.zeros((1, ROWS), F32)
        for k in range(TOP):
            node_row = node_row + jnp.where(fields_t[k : k + 1, :] == me1, fields_t[TOP + k : TOP + k + 1, :], 0.0)
        at_node_t = onehot(node_row == (iota((nodes, ROWS), 0) + 1).astype(F32))
        here_t[g] = at_node_t
        latent, slope = act(mm(got, w_emb[...]))
        d_emb[at, :] = slope.astype(BF16)
        enc, slope = act(mm(latent.astype(BF16), w_send[...]) + mm(at_node, recv_proj[...]) + length)
        d_enc[at, :] = slope.astype(BF16)
        acc[...] += mm(at_node_t, enc.astype(BF16))
        return carry

    lax.fori_loop(0, groups, encode, 0)

    upd, slope = act(mm(acc[...].astype(BF16), w_node[...]))
    d_node[...] = slope
    hid[0] = (state[...].astype(F32) + upd).astype(BF16)

    def swap_rims(step, to_left, to_right):
        one = pltpu.make_async_remote_copy(
            to_left, rims.at[step, 1], rim_send.at[step, 0], rim_recv.at[step, 1],
            device_id=(b, left), device_id_type=pl.DeviceIdType.MESH,
        )
        two = pltpu.make_async_remote_copy(
            to_right, rims.at[step, 0], rim_send.at[step, 1], rim_recv.at[step, 0],
            device_id=(b, right), device_id_type=pl.DeviceIdType.MESH,
        )
        one.start()
        two.start()
        return one, two

    swaps = []
    for layer in range(LAYERS):
        one, two = swap_rims(layer, hid.at[layer, pl.ds(0, RIM), :], hid.at[layer, pl.ds(nodes - RIM, RIM), :])
        swaps += [one, two]
        now = hid[layer]
        recv_p = mm(now, proc[layer, 1])
        send_p[0:nodes, :] = mm(now, proc[layer, 0]).astype(BF16)
        one.wait_recv()
        two.wait_recv()
        send_p[nodes : nodes + RIM, :] = mm(rims[layer, 0], proc[layer, 0]).astype(BF16)
        send_p[nodes + RIM : nodes + 2 * RIM, :] = mm(rims[layer, 1], proc[layer, 0]).astype(BF16)
        for k in range(DEG):
            at = slice(k * nodes, (k + 1) * nodes)
            out, slope = act(recv_p + mm(chosen[at, :], send_p[...]))
            d_proc[layer, at, :] = slope.astype(BF16)
            acc[...] = out if k == 0 else acc[...] + out
        upd, slope = act(mm((acc[...] * (1.0 / DEG)).astype(BF16), proc[layer, 2]))
        d_upd[layer] = slope
        after = (now.astype(F32) + upd).astype(BF16)
        if layer + 1 < LAYERS:
            hid[layer + 1] = after
        else:
            mesh_out[...] = after

    grad[...] = cot[...].astype(F32)
    for layer in reversed(range(LAYERS)):
        mean = mm((grad[...] * d_upd[layer]).astype(BF16), proc_t[layer, 2]) * (1.0 / DEG)
        for k in range(DEG):
            at = slice(k * nodes, (k + 1) * nodes)
            part = mean * d_proc[layer, at, :].astype(F32)
            grad_pre[at, :] = part.astype(BF16)
            acc[...] = part if k == 0 else acc[...] + part
        grad_ext[layer] = mm(chosen_t[nodes : 2 * nodes, :], grad_pre[...]).astype(BF16)
        one, two = swap_rims(LAYERS + layer, grad_ext.at[layer, pl.ds(0, RIM), :], grad_ext.at[layer, pl.ds(RIM, RIM), :])
        swaps += [one, two]
        own = mm(chosen_t[0:nodes, :], grad_pre[...])
        grad[...] += mm(acc[...].astype(BF16), proc_t[layer, 1])
        one.wait_recv()
        two.wait_recv()
        rim = jnp.concatenate([rims[LAYERS + layer, 0], rims[LAYERS + layer, 1]], axis=0)
        grad[...] += mm((own + rim.astype(F32)).astype(BF16), proc_t[layer, 0])

    agg = mm((grad[...] * d_node[...]).astype(BF16), w_node_t[...]).astype(BF16)
    recv_proj[...] = agg

    def decode(g, first):
        at = pl.ds(pl.multiple_of(g * ROWS, ROWS), ROWS)
        edge = (mm(here[at, :], recv_proj[...]) * d_enc[at, :].astype(F32)).astype(BF16)
        d_enc[at, :] = edge
        emb = (mm(edge, w_send_t[...]) * d_emb[at, :].astype(F32)).astype(BF16)
        back_buf[at, :] = mm(emb, w_emb_t[...]).astype(BF16)
        send_group(g, False, first)

    def decode_more(g, carry):
        decode(g, 0)
        return carry

    decode(0, 1)
    pltpu.make_async_copy(back_buf.at[pl.ds(0, CAP), :], ret_buf.at[pl.ds(0, CAP), :], bwd_recv.at[0]).start()
    lax.fori_loop(1, groups, decode_more, 0)
    acc[...] = jnp.zeros_like(acc)

    def scatter(g, carry):
        at = pl.ds(pl.multiple_of(g * ROWS, ROWS), ROWS)
        acc[...] += mm(here_t[g], d_enc[at, :])
        return carry

    lax.fori_loop(0, groups, scatter, 0)
    mesh_grad[...] = (grad[...] + mm(acc[...].astype(BF16), w_recv_t[...])).astype(BF16)

    acc[...] = jnp.zeros_like(acc)

    def collect(g, carry):
        at = pl.ds(pl.multiple_of(g * ROWS, ROWS), ROWS)
        pltpu.make_async_copy(ret_buf.at[at, :], ret_buf.at[at, :], bwd_recv.at[g]).wait()
        acc[:, 0:WIDE] += mm(unpick[g], ret_buf[at, :])
        return carry

    lax.fori_loop(0, groups, collect, 0)
    packed_t[...] = mm_t(unit, acc[:, 0:WIDE].astype(BF16)).astype(BF16)
    grid_grad_t[...] = packed_t[0:cin, :]

    for swap in swaps:
        swap.wait_send()
    others = pl.ds(CAP, (peers - 1) * CAP)
    pltpu.make_async_copy(send_buf.at[others, :], send_buf.at[others, :], fwd_send).wait()
    pltpu.make_async_copy(back_buf.at[others, :], back_buf.at[others, :], bwd_send).wait()


def local(grid_feat, mesh_state, g2m_dest, g2m_node, g2m_dist, mesh_src, w_embed, w_send, w_recv, w_node, edge_vec, proc_weights, cotangent):
    peers = lax.axis_size(AXES)
    rows, cin = grid_feat.shape
    nodes, width = mesh_state.shape
    slots = peers * CAP
    groups = peers // GROUP
    vmem = pl.BlockSpec(memory_space=pltpu.VMEM)
    anywhere = pl.BlockSpec(memory_space=pl.ANY)
    square = pltpu.VMEM((width, width), BF16)
    stack = pltpu.VMEM((LAYERS, 3, width, width), BF16)
    tile = pltpu.VMEM((nodes, width), BF16)
    mesh_out, mesh_grad, grid_grad_t = pl.pallas_call(
        kernel,
        out_shape=(
            pltpu.VMEM((nodes, width), BF16),
            pltpu.VMEM((nodes, width), BF16),
            pltpu.VMEM((cin, rows), BF16),
        ),
        in_specs=[vmem] * 7 + [anywhere] * 6,
        out_specs=(vmem,) * 3,
        scratch_shapes=[
            tile, square, square, square, stack, tile, pltpu.VMEM((WIDE, width), BF16),
            square, square, square, stack, pltpu.VMEM((width, WIDE), BF16),
            pltpu.VMEM((16, rows), F32), pltpu.VMEM((WIDE, rows), BF16), pltpu.VMEM((rows, WIDE), BF16),
            pltpu.VMEM((peers, rows), BF16),
            pltpu.VMEM((slots, WIDE), BF16), pltpu.VMEM((slots, WIDE), BF16),
            pltpu.VMEM((slots, WIDE), BF16), pltpu.VMEM((slots, WIDE), BF16),
            pltpu.VMEM((groups, rows, ROWS), BF16),
            tile, pltpu.VMEM((slots, nodes), BF16), pltpu.VMEM((groups, nodes, ROWS), BF16),
            pltpu.VMEM((slots, width), BF16), pltpu.VMEM((slots, width), BF16),
            pltpu.VMEM((nodes, width), F32), pltpu.VMEM((nodes, width), F32),
            pltpu.VMEM((DEG * nodes, 2 * nodes), BF16), pltpu.VMEM((2 * nodes, DEG * nodes), BF16),
            pltpu.VMEM((DEG * nodes, width), F32),
            pltpu.VMEM((LAYERS, DEG * nodes, width), BF16), pltpu.VMEM((LAYERS, nodes, width), F32),
            pltpu.VMEM((LAYERS, nodes, width), BF16), pltpu.VMEM((2 * nodes, width), BF16),
            pltpu.VMEM((DEG * nodes, width), BF16), pltpu.VMEM((LAYERS, 2 * RIM, width), BF16),
            pltpu.VMEM((nodes, width), F32), pltpu.VMEM((2 * LAYERS, 2, RIM, width), BF16),
            pltpu.SemaphoreType.DMA((6,)),
            pltpu.SemaphoreType.DMA, pltpu.SemaphoreType.DMA((groups,)),
            pltpu.SemaphoreType.DMA, pltpu.SemaphoreType.DMA((groups,)),
            pltpu.SemaphoreType.DMA((2 * LAYERS, 2)), pltpu.SemaphoreType.DMA((2 * LAYERS, 2)),
            pltpu.SemaphoreType.REGULAR,
        ],
        compiler_params=pltpu.CompilerParams(
            collective_id=0, has_side_effects=True, vmem_limit_bytes=56 * 2**20
        ),
    )(
        grid_feat.T, g2m_dest.T, g2m_node.T, g2m_dist.T, mesh_src.T, w_embed, edge_vec,
        mesh_state, w_send, w_recv, w_node, proc_weights, cotangent,
    )
    return mesh_out, mesh_grad, grid_grad_t.T


def solution(mesh):
    split = P(AXES, None)
    return jax.shard_map(
        local,
        mesh=mesh,
        in_specs=(split,) * 6 + (P(),) * 6 + (split,),
        out_specs=(split,) * 3,
        check_vma=False,
    )
```

```python
import functools

import jax
import jax.numpy as jnp
from jax import lax
from jax.experimental import pallas as pl
from jax.experimental.pallas import tpu as pltpu
from jax.sharding import PartitionSpec as P

TOP = 4
DEG = 6
RIM = 128
LAYERS = 2
CAP = 16
WIDE = 256
META = 240
AXES = ("band", "patch")
F32 = jnp.float32
BF16 = jnp.bfloat16
I32 = jnp.int32
GROUP = 16
ROWS = GROUP * CAP


def mm(left, right):
    return lax.dot_general(left, right, (((1,), (0,)), ((), ())), preferred_element_type=F32)


def mm_t(left, right):
    return lax.dot_general(left, right, (((1,), (1,)), ((), ())), preferred_element_type=F32)


def act(value):
    sig = 0.5 * jnp.tanh(0.5 * value) + 0.5
    out = value * sig
    return out, sig + out * (1.0 - sig)


def iota(shape, dim):
    return lax.broadcasted_iota(I32, shape, dim)


def onehot(mask):
    return jnp.where(mask, 1.0, 0.0).astype(BF16)


def wrap(value, size):
    value = jnp.where(value >= 2 * size, value - 2 * size, value)
    return jnp.where(value >= size, value - size, value)


def kernel(
    feat_hbm, dest_hbm, node_hbm, dist_hbm, src_hbm, embed_hbm, edge_hbm,
    state_hbm, w_send_hbm, w_recv_hbm, w_node_hbm, proc_hbm, cot_hbm,
    mesh_out, mesh_grad, grid_grad_t,
    feat_t, dest_t, node_t, dist_t, src_t, w_embed, edge_vec,
    state, w_send, w_recv, w_node, proc, cot, w_emb,
    w_send_t, w_recv_t, w_node_t, proc_t, w_emb_t,
    meta, packed_t, packed, place, send_buf, recv_buf, back_buf, ret_buf, unpick,
    recv_proj, here, here_t, d_emb, d_enc, acc, d_node,
    chosen, chosen_t, pre, d_proc, d_upd, hid, send_p, grad_pre, grad_ext, grad, rims,
    load_sem, fwd_send, fwd_recv, bwd_send, bwd_recv, rim_send, rim_recv, entered,
):
    bands, patches = lax.axis_size("band"), lax.axis_size("patch")
    peers = bands * patches
    groups = peers // GROUP
    nodes, width = state.shape
    cin, rows = feat_t.shape
    b, p = lax.axis_index("band"), lax.axis_index("patch")
    left, right = wrap(p + patches - 1, patches), wrap(p + 1, patches)

    loads = [
        pltpu.make_async_copy(src, dst, load_sem.at[i])
        for i, (src, dst) in enumerate(
            [
                (state_hbm, state), (w_recv_hbm, w_recv), (w_send_hbm, w_send), (w_node_hbm, w_node), (proc_hbm, proc), (cot_hbm, cot),
                (feat_hbm, feat_t), (dest_hbm, dest_t), (node_hbm, node_t), (dist_hbm, dist_t), (src_hbm, src_t), (embed_hbm, w_embed),
                (edge_hbm, edge_vec),
            ]
        )
    ]

    barrier = pltpu.get_barrier_semaphore()

    for i in range(1, bands):
        pl.semaphore_signal(barrier, inc=1, device_id=(wrap(b + i, bands), p), device_id_type=pl.DeviceIdType.MESH)
    for i in range(1, patches):
        pl.semaphore_signal(barrier, inc=1, device_id=(b, wrap(p + i, patches)), device_id_type=pl.DeviceIdType.MESH)

    for load in loads[6:] + loads[:6]:
        load.start()
    for load in loads[6:]:
        load.wait()

    meta[...] = jnp.zeros_like(meta)
    dest = dest_t[...]
    meta[0:TOP, :] = (dest + 1).astype(F32)
    meta[TOP : 2 * TOP, :] = (node_t[...] + 1).astype(F32)
    meta[2 * TOP : 3 * TOP, :] = dist_t[...].astype(F32)
    packed_t[...] = jnp.zeros_like(packed_t)
    packed_t[0:cin, :] = feat_t[...]
    packed_t[META:WIDE, :] = meta[...].astype(BF16)
    packed[...] = packed_t[...].T
    slot = iota((peers, rows), 0)
    slot_p = slot & (patches - 1)
    slot_b = (lax.shift_right_logical(slot, 3) + 5 * slot_p) & (bands - 1)
    slot_id = ((slot_b + b) & (bands - 1)) * patches + ((slot_p + p) & (patches - 1))
    named = jnp.zeros((peers, rows), F32)
    for k in range(TOP):
        named = named + jnp.where(dest[k : k + 1, :] == slot_id, 1.0, 0.0)
    before = onehot(iota((rows, rows), 0) < iota((rows, rows), 1))
    rank = mm(named.astype(BF16), before)
    place[...] = jnp.where(named > 0.5, rank, -1.0).astype(BF16)

    def pick_group(g):
        spread = onehot(lax.shift_right_logical(iota((ROWS, peers), 0) + g * ROWS, 4) == iota((ROWS, peers), 1))
        slot_place = mm(spread, place[...])
        return onehot(slot_place == (iota((ROWS, rows), 0) & (CAP - 1)).astype(F32))

    def fill(g, carry):
        for i in range(2):
            at = pl.multiple_of((2 * g + i) * ROWS, ROWS)
            send_buf[pl.ds(at, ROWS), :] = mm(pick_group(2 * g + i), packed[...]).astype(BF16)
        return carry

    lax.fori_loop(0, 2, fill, 0)
    pl.semaphore_wait(barrier, patches + bands - 2)
    for i in range(1, bands):
        pl.semaphore_signal(entered, inc=1, device_id=(wrap(b + i, bands), p), device_id_type=pl.DeviceIdType.MESH)
    lax.fori_loop(2, 4, fill, 0)

    def send_group(g, forward, which):
        source, target = (send_buf, recv_buf) if forward else (back_buf, ret_buf)
        sent, received = (fwd_send, fwd_recv) if forward else (bwd_send, bwd_recv)
        for u in which:
            dp = u % patches
            db = 2 * g + (u // patches + 5 * dp) % bands
            if forward:
                device = (wrap(b + db, bands), wrap(p + dp, patches))
            else:
                device = (wrap(b + 3 * bands - db, bands), wrap(p + patches - dp, patches))
            rows_at = pl.ds(pl.multiple_of(g * ROWS + u * CAP, CAP), CAP)
            pltpu.make_async_remote_copy(
                source.at[rows_at, :], target.at[rows_at, :], sent, received.at[g],
                device_id=device, device_id_type=pl.DeviceIdType.MESH,
            ).start()

    def send_more(g, carry):
        send_group(g, True, others)
        return carry

    def send_column(g, carry):
        send_group(g, True, column)
        return carry

    column = (0, patches)
    others = [u for u in range(GROUP) if u not in column]
    send_group(0, True, column[1:])
    lax.fori_loop(1, groups, send_column, 0)
    pl.semaphore_wait(entered, bands - 1)
    send_group(0, True, others)
    pltpu.make_async_copy(send_buf.at[pl.ds(0, CAP), :], recv_buf.at[pl.ds(0, CAP), :], fwd_recv.at[0]).start()
    lax.fori_loop(1, groups, send_more, 0)

    w_emb[...] = jnp.zeros_like(w_emb)
    w_emb[0:cin, :] = w_embed[...]
    w_emb_t[...] = w_emb[...].T
    loads[0].wait()
    loads[1].wait()
    recv_proj[...] = mm(state[...], w_recv[...]).astype(BF16)
    w_recv_t[...] = w_recv[...].T
    loads[2].wait()
    w_send_t[...] = w_send[...].T
    loads[3].wait()
    w_node_t[...] = w_node[...].T
    loads[4].wait()
    for layer in range(LAYERS):
        for i in range(3):
            proc_t[layer, i] = proc[layer, i].T
    loads[5].wait()
    unit = onehot(iota((ROWS, ROWS), 0) == iota((ROWS, ROWS), 1))
    src = src_t[...]
    here_first = (b * patches + p) * nodes
    left_first = (b * patches + left) * nodes
    right_first = (b * patches + right) * nodes
    for k in range(DEG):
        row = src[k : k + 1, :]
        own_row = jnp.where((row >= here_first) & (row < here_first + nodes), row - here_first, -1)
        rim_row = jnp.where(
            (row >= left_first + nodes - RIM) & (row < left_first + nodes),
            row - left_first - (nodes - RIM),
            jnp.where((row >= right_first) & (row < right_first + RIM), row - right_first + RIM, -1),
        )
        e = iota((nodes, nodes), 0)
        own_t = onehot(own_row == e)
        rim_t = onehot(rim_row == e)
        cols = slice(k * nodes, (k + 1) * nodes)
        chosen_t[0:nodes, cols] = own_t
        chosen_t[nodes : 2 * nodes, cols] = rim_t
        chosen[cols, 0:nodes] = mm_t(unit, own_t).astype(BF16)
        chosen[cols, nodes : 2 * nodes] = mm_t(unit, rim_t).astype(BF16)

    def fill_unpick(g, carry):
        unpick[g] = mm_t(unit, pick_group(g)).astype(BF16)
        return carry

    lax.fori_loop(0, groups, fill_unpick, 0)

    me1 = (b * patches + p + 1).astype(F32)
    c0 = META - 128
    sel_c, sel_l = iota((128, 384), 0), iota((128, 384), 1)
    sel_k = sel_l & 127
    select = onehot((sel_k < TOP) & (sel_c == c0 + sel_k + TOP * lax.shift_right_logical(sel_l, 7)))
    select_t = onehot(iota((16, 128), 1) == c0 + iota((16, 128), 0))
    ones = jnp.ones((128, nodes), BF16)
    edges = jnp.broadcast_to(edge_vec[...].astype(F32)[None, :], (128, width)).astype(BF16)
    acc[...] = jnp.zeros_like(acc)

    def encode(g, carry):
        at = pl.ds(pl.multiple_of(g * ROWS, ROWS), ROWS)
        pltpu.make_async_copy(recv_buf.at[at, :], recv_buf.at[at, :], fwd_recv.at[g]).wait()
        got = recv_buf[at, :]
        tail = got[:, 128:256]
        fields = mm(tail, select)
        mine = fields[:, 0:128] == me1
        node = mm(jnp.where(mine, fields[:, 128:256], 0.0).astype(BF16), ones)
        length = mm(jnp.where(mine, fields[:, 256:384], 0.0).astype(BF16), edges)
        at_node = onehot(node == (iota((ROWS, nodes), 1) + 1).astype(F32))
        here[at, :] = at_node
        fields_t = mm_t(select_t, tail)
        node_row = jnp.zeros((1, ROWS), F32)
        for k in range(TOP):
            node_row = node_row + jnp.where(fields_t[k : k + 1, :] == me1, fields_t[TOP + k : TOP + k + 1, :], 0.0)
        at_node_t = onehot(node_row == (iota((nodes, ROWS), 0) + 1).astype(F32))
        here_t[g] = at_node_t
        latent, slope = act(mm(got, w_emb[...]))
        d_emb[at, :] = slope.astype(BF16)
        enc, slope = act(mm(latent.astype(BF16), w_send[...]) + mm(at_node, recv_proj[...]) + length)
        d_enc[at, :] = slope.astype(BF16)
        acc[...] += mm(at_node_t, enc.astype(BF16))
        return carry

    lax.fori_loop(0, groups, encode, 0)

    upd, slope = act(mm(acc[...].astype(BF16), w_node[...]))
    d_node[...] = slope
    hid[0] = (state[...].astype(F32) + upd).astype(BF16)

    def swap_rims(step, to_left, to_right):
        one = pltpu.make_async_remote_copy(
            to_left, rims.at[step, 1], rim_send.at[step, 0], rim_recv.at[step, 1],
            device_id=(b, left), device_id_type=pl.DeviceIdType.MESH,
        )
        two = pltpu.make_async_remote_copy(
            to_right, rims.at[step, 0], rim_send.at[step, 1], rim_recv.at[step, 0],
            device_id=(b, right), device_id_type=pl.DeviceIdType.MESH,
        )
        one.start()
        two.start()
        return one, two

    swaps = []
    for layer in range(LAYERS):
        one, two = swap_rims(layer, hid.at[layer, pl.ds(0, RIM), :], hid.at[layer, pl.ds(nodes - RIM, RIM), :])
        swaps += [one, two]
        now = hid[layer]
        recv_p = mm(now, proc[layer, 1])
        send_p[0:nodes, :] = mm(now, proc[layer, 0]).astype(BF16)
        one.wait_recv()
        two.wait_recv()
        send_p[nodes : nodes + RIM, :] = mm(rims[layer, 0], proc[layer, 0]).astype(BF16)
        send_p[nodes + RIM : nodes + 2 * RIM, :] = mm(rims[layer, 1], proc[layer, 0]).astype(BF16)
        for k in range(DEG):
            at = slice(k * nodes, (k + 1) * nodes)
            out, slope = act(recv_p + mm(chosen[at, :], send_p[...]))
            d_proc[layer, at, :] = slope.astype(BF16)
            acc[...] = out if k == 0 else acc[...] + out
        upd, slope = act(mm((acc[...] * (1.0 / DEG)).astype(BF16), proc[layer, 2]))
        d_upd[layer] = slope
        after = (now.astype(F32) + upd).astype(BF16)
        if layer + 1 < LAYERS:
            hid[layer + 1] = after
        else:
            mesh_out[...] = after

    grad[...] = cot[...].astype(F32)
    for layer in reversed(range(LAYERS)):
        mean = mm((grad[...] * d_upd[layer]).astype(BF16), proc_t[layer, 2]) * (1.0 / DEG)
        for k in range(DEG):
            at = slice(k * nodes, (k + 1) * nodes)
            part = mean * d_proc[layer, at, :].astype(F32)
            grad_pre[at, :] = part.astype(BF16)
            acc[...] = part if k == 0 else acc[...] + part
        grad_ext[layer] = mm(chosen_t[nodes : 2 * nodes, :], grad_pre[...]).astype(BF16)
        one, two = swap_rims(LAYERS + layer, grad_ext.at[layer, pl.ds(0, RIM), :], grad_ext.at[layer, pl.ds(RIM, RIM), :])
        swaps += [one, two]
        own = mm(chosen_t[0:nodes, :], grad_pre[...])
        grad[...] += mm(acc[...].astype(BF16), proc_t[layer, 1])
        one.wait_recv()
        two.wait_recv()
        rim = jnp.concatenate([rims[LAYERS + layer, 0], rims[LAYERS + layer, 1]], axis=0)
        grad[...] += mm((own + rim.astype(F32)).astype(BF16), proc_t[layer, 0])

    agg = mm((grad[...] * d_node[...]).astype(BF16), w_node_t[...]).astype(BF16)
    recv_proj[...] = agg

    def decode(g, which):
        at = pl.ds(pl.multiple_of(g * ROWS, ROWS), ROWS)
        edge = (mm(here[at, :], recv_proj[...]) * d_enc[at, :].astype(F32)).astype(BF16)
        d_enc[at, :] = edge
        emb = (mm(edge, w_send_t[...]) * d_emb[at, :].astype(F32)).astype(BF16)
        back_buf[at, :] = mm(emb, w_emb_t[...]).astype(BF16)
        send_group(g, False, which)

    def decode_more(g, carry):
        decode(g, range(GROUP))
        return carry

    decode(0, range(1, GROUP))
    pltpu.make_async_copy(back_buf.at[pl.ds(0, CAP), :], ret_buf.at[pl.ds(0, CAP), :], bwd_recv.at[0]).start()
    lax.fori_loop(1, groups, decode_more, 0)
    acc[...] = jnp.zeros_like(acc)

    def scatter(g, carry):
        at = pl.ds(pl.multiple_of(g * ROWS, ROWS), ROWS)
        acc[...] += mm(here_t[g], d_enc[at, :])
        return carry

    lax.fori_loop(0, groups, scatter, 0)
    mesh_grad[...] = (grad[...] + mm(acc[...].astype(BF16), w_recv_t[...])).astype(BF16)

    acc[...] = jnp.zeros_like(acc)

    def collect(g, carry):
        at = pl.ds(pl.multiple_of(g * ROWS, ROWS), ROWS)
        pltpu.make_async_copy(ret_buf.at[at, :], ret_buf.at[at, :], bwd_recv.at[g]).wait()
        acc[:, 0:WIDE] += mm(unpick[g], ret_buf[at, :])
        return carry

    lax.fori_loop(0, groups, collect, 0)
    packed_t[...] = mm_t(unit, acc[:, 0:WIDE].astype(BF16)).astype(BF16)
    grid_grad_t[...] = packed_t[0:cin, :]

    for swap in swaps:
        swap.wait_send()
    away = pl.ds(CAP, (peers - 1) * CAP)
    pltpu.make_async_copy(send_buf.at[away, :], send_buf.at[away, :], fwd_send).wait()
    pltpu.make_async_copy(back_buf.at[away, :], back_buf.at[away, :], bwd_send).wait()


def local(grid_feat, mesh_state, g2m_dest, g2m_node, g2m_dist, mesh_src, w_embed, w_send, w_recv, w_node, edge_vec, proc_weights, cotangent):
    peers = lax.axis_size(AXES)
    rows, cin = grid_feat.shape
    nodes, width = mesh_state.shape
    slots = peers * CAP
    groups = peers // GROUP
    vmem = pl.BlockSpec(memory_space=pltpu.VMEM)
    anywhere = pl.BlockSpec(memory_space=pl.ANY)
    square = pltpu.VMEM((width, width), BF16)
    stack = pltpu.VMEM((LAYERS, 3, width, width), BF16)
    tile = pltpu.VMEM((nodes, width), BF16)
    mesh_out, mesh_grad, grid_grad_t = pl.pallas_call(
        kernel,
        out_shape=(
            pltpu.VMEM((nodes, width), BF16),
            pltpu.VMEM((nodes, width), BF16),
            pltpu.VMEM((cin, rows), BF16),
        ),
        in_specs=[anywhere] * 13,
        out_specs=(vmem,) * 3,
        scratch_shapes=[
            pltpu.VMEM((cin, rows), BF16), pltpu.VMEM((TOP, rows), I32), pltpu.VMEM((TOP, rows), I32), pltpu.VMEM((TOP, rows), BF16),
            pltpu.VMEM((DEG, nodes), I32), pltpu.VMEM((cin, width), BF16), pltpu.VMEM((width,), BF16),
            tile, square, square, square, stack, tile, pltpu.VMEM((WIDE, width), BF16),
            square, square, square, stack, pltpu.VMEM((width, WIDE), BF16),
            pltpu.VMEM((16, rows), F32), pltpu.VMEM((WIDE, rows), BF16), pltpu.VMEM((rows, WIDE), BF16),
            pltpu.VMEM((peers, rows), BF16),
            pltpu.VMEM((slots, WIDE), BF16), pltpu.VMEM((slots, WIDE), BF16),
            pltpu.VMEM((slots, WIDE), BF16), pltpu.VMEM((slots, WIDE), BF16),
            pltpu.VMEM((groups, rows, ROWS), BF16),
            tile, pltpu.VMEM((slots, nodes), BF16), pltpu.VMEM((groups, nodes, ROWS), BF16),
            pltpu.VMEM((slots, width), BF16), pltpu.VMEM((slots, width), BF16),
            pltpu.VMEM((nodes, width), F32), pltpu.VMEM((nodes, width), F32),
            pltpu.VMEM((DEG * nodes, 2 * nodes), BF16), pltpu.VMEM((2 * nodes, DEG * nodes), BF16),
            pltpu.VMEM((DEG * nodes, width), F32),
            pltpu.VMEM((LAYERS, DEG * nodes, width), BF16), pltpu.VMEM((LAYERS, nodes, width), F32),
            pltpu.VMEM((LAYERS, nodes, width), BF16), pltpu.VMEM((2 * nodes, width), BF16),
            pltpu.VMEM((DEG * nodes, width), BF16), pltpu.VMEM((LAYERS, 2 * RIM, width), BF16),
            pltpu.VMEM((nodes, width), F32), pltpu.VMEM((2 * LAYERS, 2, RIM, width), BF16),
            pltpu.SemaphoreType.DMA((13,)),
            pltpu.SemaphoreType.DMA, pltpu.SemaphoreType.DMA((groups,)),
            pltpu.SemaphoreType.DMA, pltpu.SemaphoreType.DMA((groups,)),
            pltpu.SemaphoreType.DMA((2 * LAYERS, 2)), pltpu.SemaphoreType.DMA((2 * LAYERS, 2)),
            pltpu.SemaphoreType.REGULAR,
        ],
        compiler_params=pltpu.CompilerParams(
            collective_id=0, has_side_effects=True, vmem_limit_bytes=56 * 2**20
        ),
    )(
        grid_feat.T, g2m_dest.T, g2m_node.T, g2m_dist.T, mesh_src.T, w_embed, edge_vec,
        mesh_state, w_send, w_recv, w_node, proc_weights, cotangent,
    )
    return mesh_out, mesh_grad, grid_grad_t.T


def solution(mesh):
    split = P(AXES, None)
    return jax.shard_map(
        local,
        mesh=mesh,
        in_specs=(split,) * 6 + (P(),) * 6 + (split,),
        out_specs=(split,) * 3,
        check_vma=False,
    )
```

```python
import functools

import jax
import jax.numpy as jnp
from jax import lax
from jax.experimental import pallas as pl
from jax.experimental.pallas import tpu as pltpu
from jax.sharding import PartitionSpec as P

TOP = 4
DEG = 6
RIM = 128
LAYERS = 2
CAP = 16
WIDE = 256
META = 240
AXES = ("band", "patch")
F32 = jnp.float32
BF16 = jnp.bfloat16
I32 = jnp.int32
GROUP = 16
ROWS = GROUP * CAP


def mm(left, right):
    return lax.dot_general(left, right, (((1,), (0,)), ((), ())), preferred_element_type=F32)


def mm_t(left, right):
    return lax.dot_general(left, right, (((1,), (1,)), ((), ())), preferred_element_type=F32)


def act(value):
    sig = 0.5 * jnp.tanh(0.5 * value) + 0.5
    out = value * sig
    return out, sig + out * (1.0 - sig)


def act_half(value):
    value = value.astype(BF16)
    sig = 0.5 * jnp.tanh(0.5 * value) + 0.5
    out = value * sig
    return out, sig + out * (1.0 - sig)


def iota(shape, dim):
    return lax.broadcasted_iota(I32, shape, dim)


def onehot(mask):
    return jnp.where(mask, 1.0, 0.0).astype(BF16)


def wrap(value, size):
    value = jnp.where(value >= 2 * size, value - 2 * size, value)
    return jnp.where(value >= size, value - size, value)


def kernel(
    feat_hbm, dest_hbm, node_hbm, dist_hbm, src_hbm, embed_hbm, edge_hbm,
    state_hbm, w_send_hbm, w_recv_hbm, w_node_hbm, proc_hbm, cot_hbm,
    mesh_out, mesh_grad, grid_grad_t,
    feat_t, dest_t, node_t, dist_t, src_t, w_embed, edge_vec,
    state, w_send, w_recv, w_node, proc, cot, w_emb,
    w_send_t, w_recv_t, w_node_t, proc_t, w_emb_t,
    meta, packed_t, packed, place, send_buf, recv_buf, back_buf, ret_buf, unpick,
    recv_proj, here, here_t, d_emb, d_enc, acc, d_node,
    chosen, chosen_t, pre, d_proc, d_upd, hid, send_p, grad_pre, grad_ext, grad, rims,
    load_sem, fwd_send, fwd_recv, bwd_send, bwd_recv, rim_send, rim_recv, entered,
):
    bands, patches = lax.axis_size("band"), lax.axis_size("patch")
    peers = bands * patches
    groups = peers // GROUP
    nodes, width = state.shape
    cin, rows = feat_t.shape
    b, p = lax.axis_index("band"), lax.axis_index("patch")
    left, right = wrap(p + patches - 1, patches), wrap(p + 1, patches)

    loads = [
        pltpu.make_async_copy(src, dst, load_sem.at[i])
        for i, (src, dst) in enumerate(
            [
                (state_hbm, state), (w_recv_hbm, w_recv), (w_send_hbm, w_send), (w_node_hbm, w_node), (proc_hbm, proc), (cot_hbm, cot),
                (feat_hbm, feat_t), (dest_hbm, dest_t), (node_hbm, node_t), (dist_hbm, dist_t), (src_hbm, src_t), (embed_hbm, w_embed),
                (edge_hbm, edge_vec),
            ]
        )
    ]

    barrier = pltpu.get_barrier_semaphore()

    for i in range(1, bands):
        pl.semaphore_signal(barrier, inc=1, device_id=(wrap(b + i, bands), p), device_id_type=pl.DeviceIdType.MESH)
    for i in range(1, patches):
        pl.semaphore_signal(barrier, inc=1, device_id=(b, wrap(p + i, patches)), device_id_type=pl.DeviceIdType.MESH)

    for load in loads[6:] + loads[:6]:
        load.start()
    for load in loads[6:]:
        load.wait()

    meta[...] = jnp.zeros_like(meta)
    dest = dest_t[...]
    meta[0:TOP, :] = (dest + 1).astype(F32)
    meta[TOP : 2 * TOP, :] = (node_t[...] + 1).astype(F32)
    meta[2 * TOP : 3 * TOP, :] = dist_t[...].astype(F32)
    packed_t[...] = jnp.zeros_like(packed_t)
    packed_t[0:cin, :] = feat_t[...]
    packed_t[META:WIDE, :] = meta[...].astype(BF16)
    packed[...] = packed_t[...].T
    slot = iota((peers, rows), 0)
    slot_p = slot & (patches - 1)
    slot_b = (lax.shift_right_logical(slot, 3) + 5 * slot_p) & (bands - 1)
    slot_id = ((slot_b + b) & (bands - 1)) * patches + ((slot_p + p) & (patches - 1))
    named = jnp.zeros((peers, rows), F32)
    for k in range(TOP):
        named = named + jnp.where(dest[k : k + 1, :] == slot_id, 1.0, 0.0)
    before = onehot(iota((rows, rows), 0) < iota((rows, rows), 1))
    rank = mm(named.astype(BF16), before)
    place[...] = jnp.where(named > 0.5, rank, -1.0).astype(BF16)

    def pick_group(g):
        spread = onehot(lax.shift_right_logical(iota((ROWS, peers), 0) + g * ROWS, 4) == iota((ROWS, peers), 1))
        slot_place = mm(spread, place[...])
        return onehot(slot_place == (iota((ROWS, rows), 0) & (CAP - 1)).astype(F32))

    def fill(g, carry):
        for i in range(2):
            at = pl.multiple_of((2 * g + i) * ROWS, ROWS)
            send_buf[pl.ds(at, ROWS), :] = mm(pick_group(2 * g + i), packed[...]).astype(BF16)
        return carry

    lax.fori_loop(0, 2, fill, 0)
    pl.semaphore_wait(barrier, patches + bands - 2)
    for i in range(1, bands):
        pl.semaphore_signal(entered, inc=1, device_id=(wrap(b + i, bands), p), device_id_type=pl.DeviceIdType.MESH)
    lax.fori_loop(2, 4, fill, 0)

    def send_group(g, forward, which):
        source, target = (send_buf, recv_buf) if forward else (back_buf, ret_buf)
        sent, received = (fwd_send, fwd_recv) if forward else (bwd_send, bwd_recv)
        for u in which:
            dp = u % patches
            db = 2 * g + (u // patches + 5 * dp) % bands
            if forward:
                device = (wrap(b + db, bands), wrap(p + dp, patches))
            else:
                device = (wrap(b + 3 * bands - db, bands), wrap(p + patches - dp, patches))
            rows_at = pl.ds(pl.multiple_of(g * ROWS + u * CAP, CAP), CAP)
            pltpu.make_async_remote_copy(
                source.at[rows_at, :], target.at[rows_at, :], sent, received.at[g],
                device_id=device, device_id_type=pl.DeviceIdType.MESH,
            ).start()

    def send_more(g, carry):
        send_group(g, True, others)
        return carry

    def send_column(g, carry):
        send_group(g, True, column)
        return carry

    column = (0, patches)
    others = [u for u in range(GROUP) if u not in column]
    send_group(0, True, column[1:])
    lax.fori_loop(1, groups, send_column, 0)
    pl.semaphore_wait(entered, bands - 1)
    send_group(0, True, others)
    pltpu.make_async_copy(send_buf.at[pl.ds(0, CAP), :], recv_buf.at[pl.ds(0, CAP), :], fwd_recv.at[0]).start()
    lax.fori_loop(1, groups, send_more, 0)

    w_emb[...] = jnp.zeros_like(w_emb)
    w_emb[0:cin, :] = w_embed[...]
    w_emb_t[...] = w_emb[...].T
    loads[0].wait()
    loads[1].wait()
    recv_proj[...] = mm(state[...], w_recv[...]).astype(BF16)
    w_recv_t[...] = w_recv[...].T
    loads[2].wait()
    w_send_t[...] = w_send[...].T
    loads[3].wait()
    w_node_t[...] = w_node[...].T
    loads[4].wait()
    for layer in range(LAYERS):
        for i in range(3):
            proc_t[layer, i] = proc[layer, i].T
    loads[5].wait()
    unit = onehot(iota((ROWS, ROWS), 0) == iota((ROWS, ROWS), 1))
    src = src_t[...]
    here_first = (b * patches + p) * nodes
    left_first = (b * patches + left) * nodes
    right_first = (b * patches + right) * nodes
    for k in range(DEG):
        row = src[k : k + 1, :]
        own_row = jnp.where((row >= here_first) & (row < here_first + nodes), row - here_first, -1)
        rim_row = jnp.where(
            (row >= left_first + nodes - RIM) & (row < left_first + nodes),
            row - left_first - (nodes - RIM),
            jnp.where((row >= right_first) & (row < right_first + RIM), row - right_first + RIM, -1),
        )
        e = iota((nodes, nodes), 0)
        own_t = onehot(own_row == e)
        rim_t = onehot(rim_row == e)
        cols = slice(k * nodes, (k + 1) * nodes)
        chosen_t[0:nodes, cols] = own_t
        chosen_t[nodes : 2 * nodes, cols] = rim_t
        chosen[cols, 0:nodes] = mm_t(unit, own_t).astype(BF16)
        chosen[cols, nodes : 2 * nodes] = mm_t(unit, rim_t).astype(BF16)

    def fill_unpick(g, carry):
        unpick[g] = mm_t(unit, pick_group(g)).astype(BF16)
        return carry

    lax.fori_loop(0, groups, fill_unpick, 0)

    me1 = (b * patches + p + 1).astype(F32)
    c0 = META - 128
    sel_c, sel_l = iota((128, 384), 0), iota((128, 384), 1)
    sel_k = sel_l & 127
    select = onehot((sel_k < TOP) & (sel_c == c0 + sel_k + TOP * lax.shift_right_logical(sel_l, 7)))
    select_t = onehot(iota((16, 128), 1) == c0 + iota((16, 128), 0))
    ones = jnp.ones((128, nodes), BF16)
    edges = jnp.broadcast_to(edge_vec[...].astype(F32)[None, :], (128, width)).astype(BF16)
    acc[...] = jnp.zeros_like(acc)

    def encode(g, carry):
        at = pl.ds(pl.multiple_of(g * ROWS, ROWS), ROWS)
        pltpu.make_async_copy(recv_buf.at[at, :], recv_buf.at[at, :], fwd_recv.at[g]).wait()
        got = recv_buf[at, :]
        tail = got[:, 128:256]
        fields = mm(tail, select)
        mine = fields[:, 0:128] == me1
        node = mm(jnp.where(mine, fields[:, 128:256], 0.0).astype(BF16), ones)
        length = mm(jnp.where(mine, fields[:, 256:384], 0.0).astype(BF16), edges)
        at_node = onehot(node == (iota((ROWS, nodes), 1) + 1).astype(F32))
        here[at, :] = at_node
        fields_t = mm_t(select_t, tail)
        node_row = jnp.zeros((1, ROWS), F32)
        for k in range(TOP):
            node_row = node_row + jnp.where(fields_t[k : k + 1, :] == me1, fields_t[TOP + k : TOP + k + 1, :], 0.0)
        at_node_t = onehot(node_row == (iota((nodes, ROWS), 0) + 1).astype(F32))
        here_t[g] = at_node_t
        latent, slope = act(mm(got, w_emb[...]))
        d_emb[at, :] = slope.astype(BF16)
        enc, slope = act(mm(latent.astype(BF16), w_send[...]) + mm(at_node, recv_proj[...]) + length)
        d_enc[at, :] = slope.astype(BF16)
        acc[...] += mm(at_node_t, enc.astype(BF16))
        return carry

    lax.fori_loop(0, groups, encode, 0)

    upd, slope = act(mm(acc[...].astype(BF16), w_node[...]))
    d_node[...] = slope
    hid[0] = (state[...].astype(F32) + upd).astype(BF16)

    def swap_rims(step, to_left, to_right):
        one = pltpu.make_async_remote_copy(
            to_left, rims.at[step, 1], rim_send.at[step, 0], rim_recv.at[step, 1],
            device_id=(b, left), device_id_type=pl.DeviceIdType.MESH,
        )
        two = pltpu.make_async_remote_copy(
            to_right, rims.at[step, 0], rim_send.at[step, 1], rim_recv.at[step, 0],
            device_id=(b, right), device_id_type=pl.DeviceIdType.MESH,
        )
        one.start()
        two.start()
        return one, two

    swaps = []
    for layer in range(LAYERS):
        one, two = swap_rims(layer, hid.at[layer, pl.ds(0, RIM), :], hid.at[layer, pl.ds(nodes - RIM, RIM), :])
        swaps += [one, two]
        now = hid[layer]
        recv_p = mm(now, proc[layer, 1])
        send_p[0:nodes, :] = mm(now, proc[layer, 0]).astype(BF16)
        one.wait_recv()
        two.wait_recv()
        send_p[nodes : nodes + RIM, :] = mm(rims[layer, 0], proc[layer, 0]).astype(BF16)
        send_p[nodes + RIM : nodes + 2 * RIM, :] = mm(rims[layer, 1], proc[layer, 0]).astype(BF16)
        for k in range(DEG):
            at = slice(k * nodes, (k + 1) * nodes)
            out, d_proc[layer, at, :] = act_half(recv_p + mm(chosen[at, :], send_p[...]))
            acc[...] = out.astype(F32) if k == 0 else acc[...] + out.astype(F32)
        upd, slope = act(mm((acc[...] * (1.0 / DEG)).astype(BF16), proc[layer, 2]))
        d_upd[layer] = slope
        after = (now.astype(F32) + upd).astype(BF16)
        if layer + 1 < LAYERS:
            hid[layer + 1] = after
        else:
            mesh_out[...] = after

    grad[...] = cot[...].astype(F32)
    for layer in reversed(range(LAYERS)):
        mean = mm((grad[...] * d_upd[layer]).astype(BF16), proc_t[layer, 2]) * (1.0 / DEG)
        for k in range(DEG):
            at = slice(k * nodes, (k + 1) * nodes)
            part = mean * d_proc[layer, at, :].astype(F32)
            grad_pre[at, :] = part.astype(BF16)
            acc[...] = part if k == 0 else acc[...] + part
        grad_ext[layer] = mm(chosen_t[nodes : 2 * nodes, :], grad_pre[...]).astype(BF16)
        one, two = swap_rims(LAYERS + layer, grad_ext.at[layer, pl.ds(0, RIM), :], grad_ext.at[layer, pl.ds(RIM, RIM), :])
        swaps += [one, two]
        own = mm(chosen_t[0:nodes, :], grad_pre[...])
        grad[...] += mm(acc[...].astype(BF16), proc_t[layer, 1])
        one.wait_recv()
        two.wait_recv()
        rim = jnp.concatenate([rims[LAYERS + layer, 0], rims[LAYERS + layer, 1]], axis=0)
        grad[...] += mm((own + rim.astype(F32)).astype(BF16), proc_t[layer, 0])

    agg = mm((grad[...] * d_node[...]).astype(BF16), w_node_t[...]).astype(BF16)
    recv_proj[...] = agg

    def decode(g, which):
        at = pl.ds(pl.multiple_of(g * ROWS, ROWS), ROWS)
        edge = (mm(here[at, :], recv_proj[...]) * d_enc[at, :].astype(F32)).astype(BF16)
        d_enc[at, :] = edge
        emb = (mm(edge, w_send_t[...]) * d_emb[at, :].astype(F32)).astype(BF16)
        back_buf[at, :] = mm(emb, w_emb_t[...]).astype(BF16)
        send_group(g, False, which)

    def decode_more(g, carry):
        decode(g, range(GROUP))
        return carry

    decode(0, range(1, GROUP))
    pltpu.make_async_copy(back_buf.at[pl.ds(0, CAP), :], ret_buf.at[pl.ds(0, CAP), :], bwd_recv.at[0]).start()
    lax.fori_loop(1, groups, decode_more, 0)
    acc[...] = jnp.zeros_like(acc)

    def scatter(g, carry):
        at = pl.ds(pl.multiple_of(g * ROWS, ROWS), ROWS)
        acc[...] += mm(here_t[g], d_enc[at, :])
        return carry

    lax.fori_loop(0, groups, scatter, 0)
    mesh_grad[...] = (grad[...] + mm(acc[...].astype(BF16), w_recv_t[...])).astype(BF16)

    acc[...] = jnp.zeros_like(acc)

    def collect(g, carry):
        at = pl.ds(pl.multiple_of(g * ROWS, ROWS), ROWS)
        pltpu.make_async_copy(ret_buf.at[at, :], ret_buf.at[at, :], bwd_recv.at[g]).wait()
        acc[:, 0:WIDE] += mm(unpick[g], ret_buf[at, :])
        return carry

    lax.fori_loop(0, groups, collect, 0)
    packed_t[...] = mm_t(unit, acc[:, 0:WIDE].astype(BF16)).astype(BF16)
    grid_grad_t[...] = packed_t[0:cin, :]

    for swap in swaps:
        swap.wait_send()
    away = pl.ds(CAP, (peers - 1) * CAP)
    pltpu.make_async_copy(send_buf.at[away, :], send_buf.at[away, :], fwd_send).wait()
    pltpu.make_async_copy(back_buf.at[away, :], back_buf.at[away, :], bwd_send).wait()


def local(grid_feat, mesh_state, g2m_dest, g2m_node, g2m_dist, mesh_src, w_embed, w_send, w_recv, w_node, edge_vec, proc_weights, cotangent):
    peers = lax.axis_size(AXES)
    rows, cin = grid_feat.shape
    nodes, width = mesh_state.shape
    slots = peers * CAP
    groups = peers // GROUP
    vmem = pl.BlockSpec(memory_space=pltpu.VMEM)
    anywhere = pl.BlockSpec(memory_space=pl.ANY)
    square = pltpu.VMEM((width, width), BF16)
    stack = pltpu.VMEM((LAYERS, 3, width, width), BF16)
    tile = pltpu.VMEM((nodes, width), BF16)
    mesh_out, mesh_grad, grid_grad_t = pl.pallas_call(
        kernel,
        out_shape=(
            pltpu.VMEM((nodes, width), BF16),
            pltpu.VMEM((nodes, width), BF16),
            pltpu.VMEM((cin, rows), BF16),
        ),
        in_specs=[anywhere] * 13,
        out_specs=(vmem,) * 3,
        scratch_shapes=[
            pltpu.VMEM((cin, rows), BF16), pltpu.VMEM((TOP, rows), I32), pltpu.VMEM((TOP, rows), I32), pltpu.VMEM((TOP, rows), BF16),
            pltpu.VMEM((DEG, nodes), I32), pltpu.VMEM((cin, width), BF16), pltpu.VMEM((width,), BF16),
            tile, square, square, square, stack, tile, pltpu.VMEM((WIDE, width), BF16),
            square, square, square, stack, pltpu.VMEM((width, WIDE), BF16),
            pltpu.VMEM((16, rows), F32), pltpu.VMEM((WIDE, rows), BF16), pltpu.VMEM((rows, WIDE), BF16),
            pltpu.VMEM((peers, rows), BF16),
            pltpu.VMEM((slots, WIDE), BF16), pltpu.VMEM((slots, WIDE), BF16),
            pltpu.VMEM((slots, WIDE), BF16), pltpu.VMEM((slots, WIDE), BF16),
            pltpu.VMEM((groups, rows, ROWS), BF16),
            tile, pltpu.VMEM((slots, nodes), BF16), pltpu.VMEM((groups, nodes, ROWS), BF16),
            pltpu.VMEM((slots, width), BF16), pltpu.VMEM((slots, width), BF16),
            pltpu.VMEM((nodes, width), F32), pltpu.VMEM((nodes, width), F32),
            pltpu.VMEM((DEG * nodes, 2 * nodes), BF16), pltpu.VMEM((2 * nodes, DEG * nodes), BF16),
            pltpu.VMEM((DEG * nodes, width), F32),
            pltpu.VMEM((LAYERS, DEG * nodes, width), BF16), pltpu.VMEM((LAYERS, nodes, width), F32),
            pltpu.VMEM((LAYERS, nodes, width), BF16), pltpu.VMEM((2 * nodes, width), BF16),
            pltpu.VMEM((DEG * nodes, width), BF16), pltpu.VMEM((LAYERS, 2 * RIM, width), BF16),
            pltpu.VMEM((nodes, width), F32), pltpu.VMEM((2 * LAYERS, 2, RIM, width), BF16),
            pltpu.SemaphoreType.DMA((13,)),
            pltpu.SemaphoreType.DMA, pltpu.SemaphoreType.DMA((groups,)),
            pltpu.SemaphoreType.DMA, pltpu.SemaphoreType.DMA((groups,)),
            pltpu.SemaphoreType.DMA((2 * LAYERS, 2)), pltpu.SemaphoreType.DMA((2 * LAYERS, 2)),
            pltpu.SemaphoreType.REGULAR,
        ],
        compiler_params=pltpu.CompilerParams(
            collective_id=0, has_side_effects=True, vmem_limit_bytes=56 * 2**20
        ),
    )(
        grid_feat.T, g2m_dest.T, g2m_node.T, g2m_dist.T, mesh_src.T, w_embed, edge_vec,
        mesh_state, w_send, w_recv, w_node, proc_weights, cotangent,
    )
    return mesh_out, mesh_grad, grid_grad_t.T


def solution(mesh):
    split = P(AXES, None)
    return jax.shard_map(
        local,
        mesh=mesh,
        in_specs=(split,) * 6 + (P(),) * 6 + (split,),
        out_specs=(split,) * 3,
        check_vma=False,
    )
```

```python
import functools

import jax
import jax.numpy as jnp
from jax import lax
from jax.experimental import pallas as pl
from jax.experimental.pallas import tpu as pltpu
from jax.sharding import PartitionSpec as P

TOP = 4
DEG = 6
RIM = 128
LAYERS = 2
CAP = 16
WIDE = 256
META = 240
AXES = ("band", "patch")
F32 = jnp.float32
BF16 = jnp.bfloat16
I32 = jnp.int32
GROUP = 16
ROWS = GROUP * CAP


def mm(left, right):
    return lax.dot_general(left, right, (((1,), (0,)), ((), ())), preferred_element_type=F32)


def mm_t(left, right):
    return lax.dot_general(left, right, (((1,), (1,)), ((), ())), preferred_element_type=F32)


def act(value):
    sig = 0.5 * jnp.tanh(0.5 * value) + 0.5
    out = value * sig
    return out, sig + out * (1.0 - sig)


def act_half(value):
    value = value.astype(BF16)
    sig = 0.5 * jnp.tanh(0.5 * value) + 0.5
    out = value * sig
    return out, sig + out * (1.0 - sig)


def iota(shape, dim):
    return lax.broadcasted_iota(I32, shape, dim)


def onehot(mask):
    return jnp.where(mask, 1.0, 0.0).astype(BF16)


def wrap(value, size):
    value = jnp.where(value >= 2 * size, value - 2 * size, value)
    return jnp.where(value >= size, value - size, value)


def kernel(
    feat_hbm, dest_hbm, node_hbm, dist_hbm, src_hbm, embed_hbm, edge_hbm,
    state_hbm, w_send_hbm, w_recv_hbm, w_node_hbm, proc_hbm, cot_hbm,
    mesh_out, mesh_grad, grid_grad_t,
    feat_t, dest_t, node_t, dist_t, src_t, w_embed, edge_vec,
    state, w_send, w_recv, w_node, proc, cot, w_emb,
    w_send_t, w_recv_t, w_node_t, proc_t, w_emb_t,
    meta, packed_t, packed, place, send_buf, recv_buf, back_buf, ret_buf, unpick,
    recv_proj, here, here_t, d_emb, d_enc, acc, d_node,
    chosen, chosen_t, pre, d_proc, d_upd, hid, send_p, grad_pre, grad_ext, grad, rims,
    load_sem, fwd_send, fwd_recv, bwd_send, bwd_recv, rim_send, rim_recv, entered,
):
    bands, patches = lax.axis_size("band"), lax.axis_size("patch")
    peers = bands * patches
    groups = peers // GROUP
    nodes, width = state.shape
    cin, rows = feat_t.shape
    b, p = lax.axis_index("band"), lax.axis_index("patch")
    left, right = wrap(p + patches - 1, patches), wrap(p + 1, patches)

    loads = [
        pltpu.make_async_copy(src, dst, load_sem.at[i])
        for i, (src, dst) in enumerate(
            [
                (state_hbm, state), (w_recv_hbm, w_recv), (w_send_hbm, w_send), (w_node_hbm, w_node), (proc_hbm, proc), (cot_hbm, cot),
                (feat_hbm, feat_t), (dest_hbm, dest_t), (node_hbm, node_t), (dist_hbm, dist_t), (src_hbm, src_t), (embed_hbm, w_embed),
                (edge_hbm, edge_vec),
            ]
        )
    ]

    barrier = pltpu.get_barrier_semaphore()

    for i in range(1, bands):
        pl.semaphore_signal(barrier, inc=1, device_id=(wrap(b + i, bands), p), device_id_type=pl.DeviceIdType.MESH)
    for i in range(1, patches):
        pl.semaphore_signal(barrier, inc=1, device_id=(b, wrap(p + i, patches)), device_id_type=pl.DeviceIdType.MESH)

    for load in loads[6:] + loads[:6]:
        load.start()
    for load in loads[6:]:
        load.wait()

    meta[...] = jnp.zeros_like(meta)
    dest = dest_t[...]
    meta[0:TOP, :] = (dest + 1).astype(F32)
    meta[TOP : 2 * TOP, :] = (node_t[...] + 1).astype(F32)
    meta[2 * TOP : 3 * TOP, :] = dist_t[...].astype(F32)
    packed_t[...] = jnp.zeros_like(packed_t)
    packed_t[0:cin, :] = feat_t[...]
    packed_t[META:WIDE, :] = meta[...].astype(BF16)
    packed[...] = packed_t[...].T
    slot = iota((peers, rows), 0)
    slot_p = slot & (patches - 1)
    slot_b = (lax.shift_right_logical(slot, 3) + 5 * slot_p) & (bands - 1)
    slot_id = ((slot_b + b) & (bands - 1)) * patches + ((slot_p + p) & (patches - 1))
    named = jnp.zeros((peers, rows), F32)
    for k in range(TOP):
        named = named + jnp.where(dest[k : k + 1, :] == slot_id, 1.0, 0.0)
    before = onehot(iota((rows, rows), 0) < iota((rows, rows), 1))
    rank = mm(named.astype(BF16), before)
    place[...] = jnp.where(named > 0.5, rank, -1.0).astype(BF16)

    def pick_group(g):
        spread = onehot(lax.shift_right_logical(iota((ROWS, peers), 0) + g * ROWS, 4) == iota((ROWS, peers), 1))
        slot_place = mm(spread, place[...])
        return onehot(slot_place == (iota((ROWS, rows), 0) & (CAP - 1)).astype(F32))

    def fill(g, carry):
        for i in range(2):
            at = pl.multiple_of((2 * g + i) * ROWS, ROWS)
            send_buf[pl.ds(at, ROWS), :] = mm(pick_group(2 * g + i), packed[...]).astype(BF16)
        return carry

    lax.fori_loop(0, 2, fill, 0)
    pl.semaphore_wait(barrier, patches + bands - 2)
    for i in range(1, bands):
        pl.semaphore_signal(entered, inc=1, device_id=(wrap(b + i, bands), p), device_id_type=pl.DeviceIdType.MESH)
    lax.fori_loop(2, 4, fill, 0)

    def send_group(g, forward, which):
        source, target = (send_buf, recv_buf) if forward else (back_buf, ret_buf)
        sent, received = (fwd_send, fwd_recv) if forward else (bwd_send, bwd_recv)
        for u in which:
            dp = u % patches
            db = 2 * g + (u // patches + 5 * dp) % bands
            if forward:
                device = (wrap(b + db, bands), wrap(p + dp, patches))
            else:
                device = (wrap(b + 3 * bands - db, bands), wrap(p + patches - dp, patches))
            rows_at = pl.ds(pl.multiple_of(g * ROWS + u * CAP, CAP), CAP)
            pltpu.make_async_remote_copy(
                source.at[rows_at, :], target.at[rows_at, :], sent, received.at[g],
                device_id=device, device_id_type=pl.DeviceIdType.MESH,
            ).start()

    def send_more(g, carry):
        send_group(g, True, others)
        return carry

    def send_column(g, carry):
        send_group(g, True, column)
        return carry

    column = (0, patches)
    others = [u for u in range(GROUP) if u not in column]
    send_group(0, True, column[1:])
    lax.fori_loop(1, groups, send_column, 0)
    pl.semaphore_wait(entered, bands - 1)
    send_group(0, True, others)
    pltpu.make_async_copy(send_buf.at[pl.ds(0, CAP), :], recv_buf.at[pl.ds(0, CAP), :], fwd_recv.at[0]).start()
    lax.fori_loop(1, groups, send_more, 0)

    w_emb[...] = jnp.zeros_like(w_emb)
    w_emb[0:cin, :] = w_embed[...]
    w_emb_t[...] = w_emb[...].T
    loads[0].wait()
    loads[1].wait()
    recv_proj[...] = mm(state[...], w_recv[...]).astype(BF16)
    w_recv_t[...] = w_recv[...].T
    loads[2].wait()
    w_send_t[...] = w_send[...].T
    loads[3].wait()
    w_node_t[...] = w_node[...].T
    loads[4].wait()
    for layer in range(LAYERS):
        for i in range(3):
            proc_t[layer, i] = proc[layer, i].T
    loads[5].wait()
    unit = onehot(iota((ROWS, ROWS), 0) == iota((ROWS, ROWS), 1))
    src = src_t[...]
    here_first = (b * patches + p) * nodes
    left_first = (b * patches + left) * nodes
    right_first = (b * patches + right) * nodes
    for k in range(DEG):
        row = src[k : k + 1, :]
        own_row = jnp.where((row >= here_first) & (row < here_first + nodes), row - here_first, -1)
        rim_row = jnp.where(
            (row >= left_first + nodes - RIM) & (row < left_first + nodes),
            row - left_first - (nodes - RIM),
            jnp.where((row >= right_first) & (row < right_first + RIM), row - right_first + RIM, -1),
        )
        e = iota((nodes, nodes), 0)
        own_t = onehot(own_row == e)
        rim_t = onehot(rim_row == e)
        cols = slice(k * nodes, (k + 1) * nodes)
        chosen_t[0:nodes, cols] = own_t
        chosen_t[nodes : 2 * nodes, cols] = rim_t
        chosen[cols, 0:nodes] = mm_t(unit, own_t).astype(BF16)
        chosen[cols, nodes : 2 * nodes] = mm_t(unit, rim_t).astype(BF16)

    def fill_unpick(g, carry):
        unpick[g] = mm_t(unit, pick_group(g)).astype(BF16)
        return carry

    lax.fori_loop(0, groups, fill_unpick, 0)

    me1 = (b * patches + p + 1).astype(F32)
    c0 = META - 128
    sel_c, sel_l = iota((128, 384), 0), iota((128, 384), 1)
    sel_k = sel_l & 127
    select = onehot((sel_k < TOP) & (sel_c == c0 + sel_k + TOP * lax.shift_right_logical(sel_l, 7)))
    select_t = onehot(iota((16, 128), 1) == c0 + iota((16, 128), 0))
    ones = jnp.ones((128, nodes), BF16)
    edges = jnp.broadcast_to(edge_vec[...].astype(F32)[None, :], (128, width)).astype(BF16)
    acc[...] = jnp.zeros_like(acc)

    def encode(g, carry):
        at = pl.ds(pl.multiple_of(g * ROWS, ROWS), ROWS)
        pltpu.make_async_copy(recv_buf.at[at, :], recv_buf.at[at, :], fwd_recv.at[g]).wait()
        got = recv_buf[at, :]
        tail = got[:, 128:256]
        fields = mm(tail, select)
        mine = fields[:, 0:128] == me1
        node = mm(jnp.where(mine, fields[:, 128:256], 0.0).astype(BF16), ones)
        length = mm(jnp.where(mine, fields[:, 256:384], 0.0).astype(BF16), edges)
        at_node = onehot(node == (iota((ROWS, nodes), 1) + 1).astype(F32))
        here[at, :] = at_node
        fields_t = mm_t(select_t, tail)
        node_row = jnp.zeros((1, ROWS), F32)
        for k in range(TOP):
            node_row = node_row + jnp.where(fields_t[k : k + 1, :] == me1, fields_t[TOP + k : TOP + k + 1, :], 0.0)
        at_node_t = onehot(node_row == (iota((nodes, ROWS), 0) + 1).astype(F32))
        here_t[g] = at_node_t
        latent, d_emb[at, :] = act_half(mm(got, w_emb[...]))
        enc, d_enc[at, :] = act_half(mm(latent, w_send[...]) + mm(at_node, recv_proj[...]) + length)
        acc[...] += mm(at_node_t, enc)
        return carry

    lax.fori_loop(0, groups, encode, 0)

    upd, slope = act(mm(acc[...].astype(BF16), w_node[...]))
    d_node[...] = slope
    hid[0] = (state[...].astype(F32) + upd).astype(BF16)

    def swap_rims(step, to_left, to_right):
        one = pltpu.make_async_remote_copy(
            to_left, rims.at[step, 1], rim_send.at[step, 0], rim_recv.at[step, 1],
            device_id=(b, left), device_id_type=pl.DeviceIdType.MESH,
        )
        two = pltpu.make_async_remote_copy(
            to_right, rims.at[step, 0], rim_send.at[step, 1], rim_recv.at[step, 0],
            device_id=(b, right), device_id_type=pl.DeviceIdType.MESH,
        )
        one.start()
        two.start()
        return one, two

    swaps = []
    for layer in range(LAYERS):
        one, two = swap_rims(layer, hid.at[layer, pl.ds(0, RIM), :], hid.at[layer, pl.ds(nodes - RIM, RIM), :])
        swaps += [one, two]
        now = hid[layer]
        recv_p = mm(now, proc[layer, 1])
        send_p[0:nodes, :] = mm(now, proc[layer, 0]).astype(BF16)
        one.wait_recv()
        two.wait_recv()
        send_p[nodes : nodes + RIM, :] = mm(rims[layer, 0], proc[layer, 0]).astype(BF16)
        send_p[nodes + RIM : nodes + 2 * RIM, :] = mm(rims[layer, 1], proc[layer, 0]).astype(BF16)
        for k in range(DEG):
            at = slice(k * nodes, (k + 1) * nodes)
            out, d_proc[layer, at, :] = act_half(recv_p + mm(chosen[at, :], send_p[...]))
            acc[...] = out.astype(F32) if k == 0 else acc[...] + out.astype(F32)
        upd, slope = act(mm((acc[...] * (1.0 / DEG)).astype(BF16), proc[layer, 2]))
        d_upd[layer] = slope
        after = (now.astype(F32) + upd).astype(BF16)
        if layer + 1 < LAYERS:
            hid[layer + 1] = after
        else:
            mesh_out[...] = after

    grad[...] = cot[...].astype(F32)
    for layer in reversed(range(LAYERS)):
        mean = mm((grad[...] * d_upd[layer]).astype(BF16), proc_t[layer, 2]) * (1.0 / DEG)
        for k in range(DEG):
            at = slice(k * nodes, (k + 1) * nodes)
            part = mean * d_proc[layer, at, :].astype(F32)
            grad_pre[at, :] = part.astype(BF16)
            acc[...] = part if k == 0 else acc[...] + part
        grad_ext[layer] = mm(chosen_t[nodes : 2 * nodes, :], grad_pre[...]).astype(BF16)
        one, two = swap_rims(LAYERS + layer, grad_ext.at[layer, pl.ds(0, RIM), :], grad_ext.at[layer, pl.ds(RIM, RIM), :])
        swaps += [one, two]
        own = mm(chosen_t[0:nodes, :], grad_pre[...])
        grad[...] += mm(acc[...].astype(BF16), proc_t[layer, 1])
        one.wait_recv()
        two.wait_recv()
        rim = jnp.concatenate([rims[LAYERS + layer, 0], rims[LAYERS + layer, 1]], axis=0)
        grad[...] += mm((own + rim.astype(F32)).astype(BF16), proc_t[layer, 0])

    agg = mm((grad[...] * d_node[...]).astype(BF16), w_node_t[...]).astype(BF16)
    recv_proj[...] = agg

    def decode(g, which):
        at = pl.ds(pl.multiple_of(g * ROWS, ROWS), ROWS)
        edge = (mm(here[at, :], recv_proj[...]) * d_enc[at, :].astype(F32)).astype(BF16)
        d_enc[at, :] = edge
        emb = (mm(edge, w_send_t[...]) * d_emb[at, :].astype(F32)).astype(BF16)
        back_buf[at, :] = mm(emb, w_emb_t[...]).astype(BF16)
        send_group(g, False, which)

    def decode_more(g, carry):
        decode(g, range(GROUP))
        return carry

    decode(0, range(1, GROUP))
    pltpu.make_async_copy(back_buf.at[pl.ds(0, CAP), :], ret_buf.at[pl.ds(0, CAP), :], bwd_recv.at[0]).start()
    lax.fori_loop(1, groups, decode_more, 0)
    acc[...] = jnp.zeros_like(acc)

    def scatter(g, carry):
        at = pl.ds(pl.multiple_of(g * ROWS, ROWS), ROWS)
        acc[...] += mm(here_t[g], d_enc[at, :])
        return carry

    lax.fori_loop(0, groups, scatter, 0)
    mesh_grad[...] = (grad[...] + mm(acc[...].astype(BF16), w_recv_t[...])).astype(BF16)

    acc[...] = jnp.zeros_like(acc)

    def collect(g, carry):
        at = pl.ds(pl.multiple_of(g * ROWS, ROWS), ROWS)
        pltpu.make_async_copy(ret_buf.at[at, :], ret_buf.at[at, :], bwd_recv.at[g]).wait()
        acc[:, 0:WIDE] += mm(unpick[g], ret_buf[at, :])
        return carry

    lax.fori_loop(0, groups, collect, 0)
    packed_t[...] = mm_t(unit, acc[:, 0:WIDE].astype(BF16)).astype(BF16)
    grid_grad_t[...] = packed_t[0:cin, :]

    for swap in swaps:
        swap.wait_send()
    away = pl.ds(CAP, (peers - 1) * CAP)
    pltpu.make_async_copy(send_buf.at[away, :], send_buf.at[away, :], fwd_send).wait()
    pltpu.make_async_copy(back_buf.at[away, :], back_buf.at[away, :], bwd_send).wait()


def local(grid_feat, mesh_state, g2m_dest, g2m_node, g2m_dist, mesh_src, w_embed, w_send, w_recv, w_node, edge_vec, proc_weights, cotangent):
    peers = lax.axis_size(AXES)
    rows, cin = grid_feat.shape
    nodes, width = mesh_state.shape
    slots = peers * CAP
    groups = peers // GROUP
    vmem = pl.BlockSpec(memory_space=pltpu.VMEM)
    anywhere = pl.BlockSpec(memory_space=pl.ANY)
    square = pltpu.VMEM((width, width), BF16)
    stack = pltpu.VMEM((LAYERS, 3, width, width), BF16)
    tile = pltpu.VMEM((nodes, width), BF16)
    mesh_out, mesh_grad, grid_grad_t = pl.pallas_call(
        kernel,
        out_shape=(
            pltpu.VMEM((nodes, width), BF16),
            pltpu.VMEM((nodes, width), BF16),
            pltpu.VMEM((cin, rows), BF16),
        ),
        in_specs=[anywhere] * 13,
        out_specs=(vmem,) * 3,
        scratch_shapes=[
            pltpu.VMEM((cin, rows), BF16), pltpu.VMEM((TOP, rows), I32), pltpu.VMEM((TOP, rows), I32), pltpu.VMEM((TOP, rows), BF16),
            pltpu.VMEM((DEG, nodes), I32), pltpu.VMEM((cin, width), BF16), pltpu.VMEM((width,), BF16),
            tile, square, square, square, stack, tile, pltpu.VMEM((WIDE, width), BF16),
            square, square, square, stack, pltpu.VMEM((width, WIDE), BF16),
            pltpu.VMEM((16, rows), F32), pltpu.VMEM((WIDE, rows), BF16), pltpu.VMEM((rows, WIDE), BF16),
            pltpu.VMEM((peers, rows), BF16),
            pltpu.VMEM((slots, WIDE), BF16), pltpu.VMEM((slots, WIDE), BF16),
            pltpu.VMEM((slots, WIDE), BF16), pltpu.VMEM((slots, WIDE), BF16),
            pltpu.VMEM((groups, rows, ROWS), BF16),
            tile, pltpu.VMEM((slots, nodes), BF16), pltpu.VMEM((groups, nodes, ROWS), BF16),
            pltpu.VMEM((slots, width), BF16), pltpu.VMEM((slots, width), BF16),
            pltpu.VMEM((nodes, width), F32), pltpu.VMEM((nodes, width), F32),
            pltpu.VMEM((DEG * nodes, 2 * nodes), BF16), pltpu.VMEM((2 * nodes, DEG * nodes), BF16),
            pltpu.VMEM((DEG * nodes, width), F32),
            pltpu.VMEM((LAYERS, DEG * nodes, width), BF16), pltpu.VMEM((LAYERS, nodes, width), F32),
            pltpu.VMEM((LAYERS, nodes, width), BF16), pltpu.VMEM((2 * nodes, width), BF16),
            pltpu.VMEM((DEG * nodes, width), BF16), pltpu.VMEM((LAYERS, 2 * RIM, width), BF16),
            pltpu.VMEM((nodes, width), F32), pltpu.VMEM((2 * LAYERS, 2, RIM, width), BF16),
            pltpu.SemaphoreType.DMA((13,)),
            pltpu.SemaphoreType.DMA, pltpu.SemaphoreType.DMA((groups,)),
            pltpu.SemaphoreType.DMA, pltpu.SemaphoreType.DMA((groups,)),
            pltpu.SemaphoreType.DMA((2 * LAYERS, 2)), pltpu.SemaphoreType.DMA((2 * LAYERS, 2)),
            pltpu.SemaphoreType.REGULAR,
        ],
        compiler_params=pltpu.CompilerParams(
            collective_id=0, has_side_effects=True, vmem_limit_bytes=56 * 2**20
        ),
    )(
        grid_feat.T, g2m_dest.T, g2m_node.T, g2m_dist.T, mesh_src.T, w_embed, edge_vec,
        mesh_state, w_send, w_recv, w_node, proc_weights, cotangent,
    )
    return mesh_out, mesh_grad, grid_grad_t.T


def solution(mesh):
    split = P(AXES, None)
    return jax.shard_map(
        local,
        mesh=mesh,
        in_specs=(split,) * 6 + (P(),) * 6 + (split,),
        out_specs=(split,) * 3,
        check_vma=False,
    )
```

```python
import functools

import jax
import jax.numpy as jnp
from jax import lax
from jax.experimental import pallas as pl
from jax.experimental.pallas import tpu as pltpu
from jax.sharding import PartitionSpec as P

TOP = 4
DEG = 6
RIM = 128
LAYERS = 2
CAP = 16
WIDE = 256
META = 240
AXES = ("band", "patch")
F32 = jnp.float32
BF16 = jnp.bfloat16
I32 = jnp.int32
GROUP = 16
ROWS = GROUP * CAP


def mm(left, right):
    return lax.dot_general(left, right, (((1,), (0,)), ((), ())), preferred_element_type=F32)


def mm_t(left, right):
    return lax.dot_general(left, right, (((1,), (1,)), ((), ())), preferred_element_type=F32)


def act(value):
    sig = 0.5 * jnp.tanh(0.5 * value) + 0.5
    out = value * sig
    return out, sig + out * (1.0 - sig)


def act_half(value):
    value = value.astype(BF16)
    sig = 0.5 * jnp.tanh(0.5 * value) + 0.5
    out = value * sig
    return out, sig + out * (1.0 - sig)


def iota(shape, dim):
    return lax.broadcasted_iota(I32, shape, dim)


def onehot(mask):
    return jnp.where(mask, 1.0, 0.0).astype(BF16)


def wrap(value, size):
    value = jnp.where(value >= 2 * size, value - 2 * size, value)
    return jnp.where(value >= size, value - size, value)


def kernel(
    feat_hbm, dest_hbm, node_hbm, dist_hbm, src_hbm, embed_hbm, edge_hbm,
    state_hbm, w_send_hbm, w_recv_hbm, w_node_hbm, proc_hbm, cot_hbm,
    mesh_out, mesh_grad, grid_grad_t,
    feat_t, dest_t, node_t, dist_t, src_t, w_embed, edge_vec,
    state, w_send, w_recv, w_node, proc, cot, w_emb,
    w_send_t, w_recv_t, w_node_t, proc_t, w_emb_t,
    meta, packed_t, packed, place, send_buf, recv_buf, back_buf, ret_buf, unpick,
    recv_proj, here, here_t, d_emb, d_enc, acc, d_node,
    chosen, chosen_t, pre, d_proc, d_upd, hid, send_p, grad_pre, grad_ext, grad, rims,
    load_sem, fwd_send, fwd_recv, bwd_send, bwd_recv, rim_send, rim_recv, entered,
):
    bands, patches = lax.axis_size("band"), lax.axis_size("patch")
    peers = bands * patches
    groups = peers // GROUP
    nodes, width = state.shape
    cin, rows = feat_t.shape
    b, p = lax.axis_index("band"), lax.axis_index("patch")
    left, right = wrap(p + patches - 1, patches), wrap(p + 1, patches)

    loads = [
        pltpu.make_async_copy(src, dst, load_sem.at[i])
        for i, (src, dst) in enumerate(
            [
                (state_hbm, state), (w_recv_hbm, w_recv), (w_send_hbm, w_send), (w_node_hbm, w_node), (proc_hbm, proc), (cot_hbm, cot),
                (feat_hbm, feat_t), (dest_hbm, dest_t), (node_hbm, node_t), (dist_hbm, dist_t), (src_hbm, src_t), (embed_hbm, w_embed),
                (edge_hbm, edge_vec),
            ]
        )
    ]

    barrier = pltpu.get_barrier_semaphore()

    for i in range(1, bands):
        pl.semaphore_signal(barrier, inc=1, device_id=(wrap(b + i, bands), p), device_id_type=pl.DeviceIdType.MESH)
    for i in range(1, patches):
        pl.semaphore_signal(barrier, inc=1, device_id=(b, wrap(p + i, patches)), device_id_type=pl.DeviceIdType.MESH)

    for load in loads[6:] + loads[:6]:
        load.start()
    for load in loads[6:]:
        load.wait()

    meta[...] = jnp.zeros_like(meta)
    dest = dest_t[...]
    meta[0:TOP, :] = (dest + 1).astype(F32)
    meta[TOP : 2 * TOP, :] = (node_t[...] + 1).astype(F32)
    meta[2 * TOP : 3 * TOP, :] = dist_t[...].astype(F32)
    packed_t[...] = jnp.zeros_like(packed_t)
    packed_t[0:cin, :] = feat_t[...]
    packed_t[META:WIDE, :] = meta[...].astype(BF16)
    packed[...] = packed_t[...].T
    slot = iota((peers, rows), 0)
    slot_p = slot & (patches - 1)
    slot_b = (lax.shift_right_logical(slot, 3) + 5 * slot_p) & (bands - 1)
    slot_id = ((slot_b + b) & (bands - 1)) * patches + ((slot_p + p) & (patches - 1))
    named = jnp.zeros((peers, rows), F32)
    for k in range(TOP):
        named = named + jnp.where(dest[k : k + 1, :] == slot_id, 1.0, 0.0)
    before = onehot(iota((rows, rows), 0) < iota((rows, rows), 1))
    rank = mm(named.astype(BF16), before)
    place[...] = jnp.where(named > 0.5, rank, -1.0).astype(BF16)

    def pick_group(g):
        spread = onehot(lax.shift_right_logical(iota((ROWS, peers), 0) + g * ROWS, 4) == iota((ROWS, peers), 1))
        slot_place = mm(spread, place[...])
        return onehot(slot_place == (iota((ROWS, rows), 0) & (CAP - 1)).astype(F32))

    def fill(g, carry):
        for i in range(2):
            at = pl.multiple_of((2 * g + i) * ROWS, ROWS)
            send_buf[pl.ds(at, ROWS), :] = mm(pick_group(2 * g + i), packed[...]).astype(BF16)
        return carry

    lax.fori_loop(0, 2, fill, 0)
    pl.semaphore_wait(barrier, patches + bands - 2)
    for i in range(1, bands):
        pl.semaphore_signal(entered, inc=1, device_id=(wrap(b + i, bands), p), device_id_type=pl.DeviceIdType.MESH)
    lax.fori_loop(2, 4, fill, 0)

    def send_group(g, forward, which):
        source, target = (send_buf, recv_buf) if forward else (back_buf, ret_buf)
        sent, received = (fwd_send, fwd_recv) if forward else (bwd_send, bwd_recv)
        for u in which:
            dp = u % patches
            db = 2 * g + (u // patches + 5 * dp) % bands
            if forward:
                device = (wrap(b + db, bands), wrap(p + dp, patches))
            else:
                device = (wrap(b + 3 * bands - db, bands), wrap(p + patches - dp, patches))
            rows_at = pl.ds(pl.multiple_of(g * ROWS + u * CAP, CAP), CAP)
            pltpu.make_async_remote_copy(
                source.at[rows_at, :], target.at[rows_at, :], sent, received.at[g],
                device_id=device, device_id_type=pl.DeviceIdType.MESH,
            ).start()

    def send_more(g, carry):
        send_group(g, True, others)
        return carry

    def send_column(g, carry):
        send_group(g, True, column)
        return carry

    column = (0, patches)
    others = [u for u in range(GROUP) if u not in column]
    send_group(0, True, column[1:])
    lax.fori_loop(1, groups, send_column, 0)
    pl.semaphore_wait(entered, bands - 1)
    send_group(0, True, others)
    pltpu.make_async_copy(send_buf.at[pl.ds(0, CAP), :], recv_buf.at[pl.ds(0, CAP), :], fwd_recv.at[0]).start()
    lax.fori_loop(1, groups, send_more, 0)

    w_emb[...] = jnp.zeros_like(w_emb)
    w_emb[0:cin, :] = w_embed[...]
    w_emb_t[...] = w_emb[...].T
    loads[0].wait()
    loads[1].wait()
    recv_proj[...] = mm(state[...], w_recv[...]).astype(BF16)
    w_recv_t[...] = w_recv[...].T
    loads[2].wait()
    w_send_t[...] = w_send[...].T
    loads[3].wait()
    w_node_t[...] = w_node[...].T
    loads[4].wait()
    for layer in range(LAYERS):
        for i in range(3):
            proc_t[layer, i] = proc[layer, i].T
    loads[5].wait()
    unit = onehot(iota((ROWS, ROWS), 0) == iota((ROWS, ROWS), 1))
    src = src_t[...]
    here_first = (b * patches + p) * nodes
    left_first = (b * patches + left) * nodes
    right_first = (b * patches + right) * nodes
    for k in range(DEG):
        row = src[k : k + 1, :]
        own_row = jnp.where((row >= here_first) & (row < here_first + nodes), row - here_first, -1)
        rim_row = jnp.where(
            (row >= left_first + nodes - RIM) & (row < left_first + nodes),
            row - left_first - (nodes - RIM),
            jnp.where((row >= right_first) & (row < right_first + RIM), row - right_first + RIM, -1),
        )
        e = iota((nodes, nodes), 0)
        own_t = onehot(own_row == e)
        rim_t = onehot(rim_row == e)
        cols = slice(k * nodes, (k + 1) * nodes)
        chosen_t[0:nodes, cols] = own_t
        chosen_t[nodes : 2 * nodes, cols] = rim_t
        chosen[cols, 0:nodes] = mm_t(unit, own_t).astype(BF16)
        chosen[cols, nodes : 2 * nodes] = mm_t(unit, rim_t).astype(BF16)

    def fill_unpick(g, carry):
        unpick[g] = mm_t(unit, pick_group(g)).astype(BF16)
        return carry

    lax.fori_loop(0, groups, fill_unpick, 0)

    me1 = (b * patches + p + 1).astype(F32)
    c0 = META - 128
    sel_c, sel_l = iota((128, 384), 0), iota((128, 384), 1)
    sel_k = sel_l & 127
    select = onehot((sel_k < TOP) & (sel_c == c0 + sel_k + TOP * lax.shift_right_logical(sel_l, 7)))
    select_t = onehot(iota((16, 128), 1) == c0 + iota((16, 128), 0))
    ones = jnp.ones((128, nodes), BF16)
    edges = jnp.broadcast_to(edge_vec[...].astype(F32)[None, :], (128, width)).astype(BF16)
    acc[...] = jnp.zeros_like(acc)

    def encode(g, carry):
        at = pl.ds(pl.multiple_of(g * ROWS, ROWS), ROWS)
        pltpu.make_async_copy(recv_buf.at[at, :], recv_buf.at[at, :], fwd_recv.at[g]).wait()
        got = recv_buf[at, :]
        tail = got[:, 128:256]
        fields = mm(tail, select)
        mine = fields[:, 0:128] == me1
        node = mm(jnp.where(mine, fields[:, 128:256], 0.0).astype(BF16), ones)
        length = mm(jnp.where(mine, fields[:, 256:384], 0.0).astype(BF16), edges)
        at_node = onehot(node == (iota((ROWS, nodes), 1) + 1).astype(F32))
        here[at, :] = at_node
        fields_t = mm_t(select_t, tail)
        node_row = jnp.zeros((1, ROWS), F32)
        for k in range(TOP):
            node_row = node_row + jnp.where(fields_t[k : k + 1, :] == me1, fields_t[TOP + k : TOP + k + 1, :], 0.0)
        at_node_t = onehot(node_row == (iota((nodes, ROWS), 0) + 1).astype(F32))
        here_t[g] = at_node_t
        latent, d_emb[at, :] = act_half(mm(got, w_emb[...]))
        enc, d_enc[at, :] = act_half(mm(latent, w_send[...]) + mm(at_node, recv_proj[...]) + length)
        acc[...] += mm(at_node_t, enc)
        return carry

    def encode_two(i, carry):
        encode(2 * i, carry)
        return encode(2 * i + 1, carry)

    lax.fori_loop(0, groups // 2, encode_two, 0)

    upd, slope = act(mm(acc[...].astype(BF16), w_node[...]))
    d_node[...] = slope
    hid[0] = (state[...].astype(F32) + upd).astype(BF16)

    def swap_rims(step, to_left, to_right):
        one = pltpu.make_async_remote_copy(
            to_left, rims.at[step, 1], rim_send.at[step, 0], rim_recv.at[step, 1],
            device_id=(b, left), device_id_type=pl.DeviceIdType.MESH,
        )
        two = pltpu.make_async_remote_copy(
            to_right, rims.at[step, 0], rim_send.at[step, 1], rim_recv.at[step, 0],
            device_id=(b, right), device_id_type=pl.DeviceIdType.MESH,
        )
        one.start()
        two.start()
        return one, two

    swaps = []
    for layer in range(LAYERS):
        one, two = swap_rims(layer, hid.at[layer, pl.ds(0, RIM), :], hid.at[layer, pl.ds(nodes - RIM, RIM), :])
        swaps += [one, two]
        now = hid[layer]
        recv_p = mm(now, proc[layer, 1])
        send_p[0:nodes, :] = mm(now, proc[layer, 0]).astype(BF16)
        one.wait_recv()
        two.wait_recv()
        send_p[nodes : nodes + RIM, :] = mm(rims[layer, 0], proc[layer, 0]).astype(BF16)
        send_p[nodes + RIM : nodes + 2 * RIM, :] = mm(rims[layer, 1], proc[layer, 0]).astype(BF16)
        for k in range(DEG):
            at = slice(k * nodes, (k + 1) * nodes)
            out, d_proc[layer, at, :] = act_half(recv_p + mm(chosen[at, :], send_p[...]))
            acc[...] = out.astype(F32) if k == 0 else acc[...] + out.astype(F32)
        upd, slope = act(mm((acc[...] * (1.0 / DEG)).astype(BF16), proc[layer, 2]))
        d_upd[layer] = slope
        after = (now.astype(F32) + upd).astype(BF16)
        if layer + 1 < LAYERS:
            hid[layer + 1] = after
        else:
            mesh_out[...] = after

    grad[...] = cot[...].astype(F32)
    for layer in reversed(range(LAYERS)):
        mean = mm((grad[...] * d_upd[layer]).astype(BF16), proc_t[layer, 2]) * (1.0 / DEG)
        for k in range(DEG):
            at = slice(k * nodes, (k + 1) * nodes)
            part = mean * d_proc[layer, at, :].astype(F32)
            grad_pre[at, :] = part.astype(BF16)
            acc[...] = part if k == 0 else acc[...] + part
        grad_ext[layer] = mm(chosen_t[nodes : 2 * nodes, :], grad_pre[...]).astype(BF16)
        one, two = swap_rims(LAYERS + layer, grad_ext.at[layer, pl.ds(0, RIM), :], grad_ext.at[layer, pl.ds(RIM, RIM), :])
        swaps += [one, two]
        own = mm(chosen_t[0:nodes, :], grad_pre[...])
        grad[...] += mm(acc[...].astype(BF16), proc_t[layer, 1])
        one.wait_recv()
        two.wait_recv()
        rim = jnp.concatenate([rims[LAYERS + layer, 0], rims[LAYERS + layer, 1]], axis=0)
        grad[...] += mm((own + rim.astype(F32)).astype(BF16), proc_t[layer, 0])

    agg = mm((grad[...] * d_node[...]).astype(BF16), w_node_t[...]).astype(BF16)
    recv_proj[...] = agg

    def decode(g, which):
        at = pl.ds(pl.multiple_of(g * ROWS, ROWS), ROWS)
        edge = (mm(here[at, :], recv_proj[...]) * d_enc[at, :].astype(F32)).astype(BF16)
        d_enc[at, :] = edge
        emb = (mm(edge, w_send_t[...]) * d_emb[at, :].astype(F32)).astype(BF16)
        back_buf[at, :] = mm(emb, w_emb_t[...]).astype(BF16)
        send_group(g, False, which)

    def decode_more(g, carry):
        decode(g, range(GROUP))
        return carry

    decode(0, range(1, GROUP))
    pltpu.make_async_copy(back_buf.at[pl.ds(0, CAP), :], ret_buf.at[pl.ds(0, CAP), :], bwd_recv.at[0]).start()
    lax.fori_loop(1, groups, decode_more, 0)
    acc[...] = jnp.zeros_like(acc)

    def scatter(g, carry):
        at = pl.ds(pl.multiple_of(g * ROWS, ROWS), ROWS)
        acc[...] += mm(here_t[g], d_enc[at, :])
        return carry

    lax.fori_loop(0, groups, scatter, 0)
    mesh_grad[...] = (grad[...] + mm(acc[...].astype(BF16), w_recv_t[...])).astype(BF16)

    acc[...] = jnp.zeros_like(acc)

    def collect(g, carry):
        at = pl.ds(pl.multiple_of(g * ROWS, ROWS), ROWS)
        pltpu.make_async_copy(ret_buf.at[at, :], ret_buf.at[at, :], bwd_recv.at[g]).wait()
        acc[:, 0:WIDE] += mm(unpick[g], ret_buf[at, :])
        return carry

    lax.fori_loop(0, groups, collect, 0)
    packed_t[...] = mm_t(unit, acc[:, 0:WIDE].astype(BF16)).astype(BF16)
    grid_grad_t[...] = packed_t[0:cin, :]

    for swap in swaps:
        swap.wait_send()
    away = pl.ds(CAP, (peers - 1) * CAP)
    pltpu.make_async_copy(send_buf.at[away, :], send_buf.at[away, :], fwd_send).wait()
    pltpu.make_async_copy(back_buf.at[away, :], back_buf.at[away, :], bwd_send).wait()


def local(grid_feat, mesh_state, g2m_dest, g2m_node, g2m_dist, mesh_src, w_embed, w_send, w_recv, w_node, edge_vec, proc_weights, cotangent):
    peers = lax.axis_size(AXES)
    rows, cin = grid_feat.shape
    nodes, width = mesh_state.shape
    slots = peers * CAP
    groups = peers // GROUP
    vmem = pl.BlockSpec(memory_space=pltpu.VMEM)
    anywhere = pl.BlockSpec(memory_space=pl.ANY)
    square = pltpu.VMEM((width, width), BF16)
    stack = pltpu.VMEM((LAYERS, 3, width, width), BF16)
    tile = pltpu.VMEM((nodes, width), BF16)
    mesh_out, mesh_grad, grid_grad_t = pl.pallas_call(
        kernel,
        out_shape=(
            pltpu.VMEM((nodes, width), BF16),
            pltpu.VMEM((nodes, width), BF16),
            pltpu.VMEM((cin, rows), BF16),
        ),
        in_specs=[anywhere] * 13,
        out_specs=(vmem,) * 3,
        scratch_shapes=[
            pltpu.VMEM((cin, rows), BF16), pltpu.VMEM((TOP, rows), I32), pltpu.VMEM((TOP, rows), I32), pltpu.VMEM((TOP, rows), BF16),
            pltpu.VMEM((DEG, nodes), I32), pltpu.VMEM((cin, width), BF16), pltpu.VMEM((width,), BF16),
            tile, square, square, square, stack, tile, pltpu.VMEM((WIDE, width), BF16),
            square, square, square, stack, pltpu.VMEM((width, WIDE), BF16),
            pltpu.VMEM((16, rows), F32), pltpu.VMEM((WIDE, rows), BF16), pltpu.VMEM((rows, WIDE), BF16),
            pltpu.VMEM((peers, rows), BF16),
            pltpu.VMEM((slots, WIDE), BF16), pltpu.VMEM((slots, WIDE), BF16),
            pltpu.VMEM((slots, WIDE), BF16), pltpu.VMEM((slots, WIDE), BF16),
            pltpu.VMEM((groups, rows, ROWS), BF16),
            tile, pltpu.VMEM((slots, nodes), BF16), pltpu.VMEM((groups, nodes, ROWS), BF16),
            pltpu.VMEM((slots, width), BF16), pltpu.VMEM((slots, width), BF16),
            pltpu.VMEM((nodes, width), F32), pltpu.VMEM((nodes, width), F32),
            pltpu.VMEM((DEG * nodes, 2 * nodes), BF16), pltpu.VMEM((2 * nodes, DEG * nodes), BF16),
            pltpu.VMEM((DEG * nodes, width), F32),
            pltpu.VMEM((LAYERS, DEG * nodes, width), BF16), pltpu.VMEM((LAYERS, nodes, width), F32),
            pltpu.VMEM((LAYERS, nodes, width), BF16), pltpu.VMEM((2 * nodes, width), BF16),
            pltpu.VMEM((DEG * nodes, width), BF16), pltpu.VMEM((LAYERS, 2 * RIM, width), BF16),
            pltpu.VMEM((nodes, width), F32), pltpu.VMEM((2 * LAYERS, 2, RIM, width), BF16),
            pltpu.SemaphoreType.DMA((13,)),
            pltpu.SemaphoreType.DMA, pltpu.SemaphoreType.DMA((groups,)),
            pltpu.SemaphoreType.DMA, pltpu.SemaphoreType.DMA((groups,)),
            pltpu.SemaphoreType.DMA((2 * LAYERS, 2)), pltpu.SemaphoreType.DMA((2 * LAYERS, 2)),
            pltpu.SemaphoreType.REGULAR,
        ],
        compiler_params=pltpu.CompilerParams(
            collective_id=0, has_side_effects=True, vmem_limit_bytes=56 * 2**20
        ),
    )(
        grid_feat.T, g2m_dest.T, g2m_node.T, g2m_dist.T, mesh_src.T, w_embed, edge_vec,
        mesh_state, w_send, w_recv, w_node, proc_weights, cotangent,
    )
    return mesh_out, mesh_grad, grid_grad_t.T


def solution(mesh):
    split = P(AXES, None)
    return jax.shard_map(
        local,
        mesh=mesh,
        in_specs=(split,) * 6 + (P(),) * 6 + (split,),
        out_specs=(split,) * 3,
        check_vma=False,
    )
```
